128 devices in a mesh: lat: 4 (over y_hi, core), lon: 32 (over x, y_lo, z).
Axes of the slice: x: 4, y: 4 (y_hi: 2, y_lo: 2; y = y_hi * 2 + y_lo), z: 4, core: 2. Of those that a mesh axis runs over, the one named last changes fastest.
Arguments:
- query_states: bfloat16 [16384, 512], P(('lat', 'lon')), may hold values from -41 to 41
- key_states: bfloat16 [16384, 512], P(('lat', 'lon')), may hold values from -17 to 17
- silu_slope: bfloat16 [16384, 2048], P(('lat', 'lon')), may hold values from -0.099609375 to 1.09375
- w_value: bfloat16 [512, 512], replicated, may hold values from -0.25 to 0.25
- w_out: bfloat16 [512, 512], replicated, may hold values from -0.5 to 0.5
- w_up: bfloat16 [512, 2048], replicated, may hold values from -0.25 to 0.25
- w_down: bfloat16 [2048, 512], replicated, may hold values from -0.125 to 0.125
- w_obs: bfloat16 [512, 128], replicated, may hold values from -0.25 to 0.25
- obs_cells: int32 [4, 32, 4, 4, 128], P('lat', 'lon'), may hold values from 0 to 127
- obs_weights: float32 [4, 32, 4, 4, 128], P('lat', 'lon'), may hold values from 0.05 to 0.5
- obs_count: int32 [4, 32, 4], P('lat', 'lon'), may hold values from 32 to 128, as said below
- innovations: float32 [4, 32, 128, 4, 128], P('lat', 'lon'), may hold values from -13 to 13
- obs_precision: float32 [128], replicated, may hold values from 0.3 to 3
Outputs:
- solution: float32 [16384, 512], P(('lat', 'lon'))
- residual: float32 [16384, 512], P(('lat', 'lon'))
The draws below stay inside these ranges and needn't reach their ends.
Inputs may be any that keep to these rules, and one draw needn't show every extreme that they name: `obs_count`: in every draw, for each longitude sector, one latitude band receives 128 live slots from every device of that sector.
All inputs are finite; a program needn't handle non-finite values.
Results may differ from the reference program's by a relative error of at most 0.034.
Values may be sent and summed in bfloat16 or wider, within the bound.
A program may use at most 128 MiB of HBM per device.

```python
import math
import jax
import jax.numpy as jnp
from jax import lax

D = 512
HEADS = 8
HEAD_DIM = 64
FF = 2048
CHANNELS = 128
STENCIL = 4
ITERS = 2
TOK_DEV = 128
SLOTS = 128
SEQ = 4096
TOKENS = 16384
N_LAT = 4
N_LON = 32


def draw_key_states(key, part):
    key = jax.random.fold_in(key, 1)
    own_rows = jnp.clip(jax.random.normal(key, (TOKENS, D), jnp.float32), -4.0, 4.0) * 1.4
    return own_rows.astype(jnp.bfloat16)


def draw_query_states(key, part):
    key = jax.random.fold_in(key, 2)
    own_rows = jnp.clip(jax.random.normal(key, (TOKENS, D), jnp.float32), -4.0, 4.0) * 1.4
    return own_rows.astype(jnp.bfloat16)


def draw_obs_count(key, part):
    key = jax.random.fold_in(key, 3)
    busiest = jax.random.randint(jax.random.fold_in(key, 1), (1, N_LON, 1), 0, N_LAT)
    counts = jax.random.randint(jax.random.fold_in(key, 2), (N_LAT, N_LON, N_LAT), SLOTS // 4, SLOTS + 1)
    dest_band = lax.broadcasted_iota(jnp.int32, (N_LAT, N_LON, N_LAT), 2)
    return jnp.where(dest_band == busiest, SLOTS, counts).astype(jnp.int32)


def draw_innovations(key, part):
    key = jax.random.fold_in(key, 4)
    shape_all = (N_LAT, N_LON, CHANNELS, N_LAT, SLOTS)
    device_rank = (lax.broadcasted_iota(jnp.int32, shape_all, 0) * N_LON + lax.broadcasted_iota(jnp.int32, shape_all, 1)).astype(jnp.float32)
    rising = 0.6 + 1.2 * device_rank / (N_LAT * N_LON - 1)
    sample = jnp.clip(jax.random.normal(jax.random.fold_in(key, 3), shape_all, jnp.float32), -4.0, 4.0)
    return sample * rising


def set_ends(array, key, least, top_value):
    place = [jax.random.randint(jax.random.fold_in(key, axis), (), 0, length) for axis, length in enumerate(array.shape)]
    main_axis = array.shape.index(max(array.shape))
    next_to = place[:main_axis] + [(place[main_axis] + 1) % array.shape[main_axis]] + place[main_axis + 1:]
    return array.at[tuple(place)].set(least).at[tuple(next_to)].set(top_value)


def shard_levels(key, dims, cuts, low, high):
    def one(dim, shards_of):
        heights = jax.random.uniform(jax.random.fold_in(jax.random.fold_in(key, 6), dim), (shards_of,), jnp.float32, low / len(cuts), high / len(cuts))
        return jnp.repeat(jnp.exp(heights), dims[dim] // shards_of).reshape((-1,) + (1,) * (len(dims) - dim - 1))

    loudness = one(*cuts[0])
    for cut in cuts[1:]:
        loudness = loudness * one(*cut)
    return loudness


def normal_values(own_key, extent, scale, limit, kind=jnp.bfloat16):
    values = jax.random.normal(own_key, extent, jnp.float32) * scale
    return jnp.minimum(jnp.maximum(values, -limit), limit).astype(kind)


def setup_inputs(seed: int = 0) -> dict:
    arg_keys = jax.random.split(jax.random.key(seed), 14)
    query_states = draw_query_states(jax.random.fold_in(arg_keys[13], 71), 0)
    key_states = draw_key_states(jax.random.fold_in(arg_keys[13], 71), 0)
    silu_slope = jnp.clip(-0.099609375 + 1.1933594 * jax.random.uniform(arg_keys[2], (TOKENS, FF), jnp.float32) ** shard_levels(arg_keys[2], (TOKENS, FF), ((0, 128),), -0.2, 0.2), -0.099609375, 1.09375).astype(jnp.bfloat16)
    w_value = normal_values(arg_keys[3], (D, D), D ** -0.5, 0.25)
    w_out = normal_values(arg_keys[4], (D, D), (D // 4) ** -0.5, 0.5)
    w_up = normal_values(arg_keys[5], (D, FF), D ** -0.5, 0.25)
    w_down = normal_values(arg_keys[6], (FF, D), FF ** -0.5, 0.125)
    w_obs = normal_values(arg_keys[7], (D, CHANNELS), D ** -0.5, 0.25)
    obs_cells = set_ends(jax.random.randint(arg_keys[8], (N_LAT, N_LON, STENCIL, N_LAT, SLOTS), 0, TOK_DEV), jax.random.fold_in(arg_keys[8], 1), 0, TOK_DEV - 1).astype(jnp.int32)
    obs_weights = jnp.clip(0.05 + 0.45 * jax.random.uniform(arg_keys[9], (N_LAT, N_LON, STENCIL, N_LAT, SLOTS), jnp.float32) ** shard_levels(arg_keys[9], (N_LAT, N_LON, STENCIL, N_LAT, SLOTS), ((0, 4), (1, 32)), -0.2, 0.2), 0.05, 0.5)
    obs_count = draw_obs_count(jax.random.fold_in(arg_keys[13], 71), 0)
    innovations = draw_innovations(jax.random.fold_in(arg_keys[13], 71), 0)
    obs_precision = jnp.clip(jnp.exp(jax.random.uniform(arg_keys[12], (CHANNELS,), jnp.float32, math.log(0.3), math.log(3.0))), 0.3, 3.0)
    return dict(query_states=query_states, key_states=key_states, silu_slope=silu_slope, w_value=w_value, w_out=w_out, w_up=w_up, w_down=w_down, w_obs=w_obs, obs_cells=obs_cells, obs_weights=obs_weights, obs_count=obs_count, innovations=innovations, obs_precision=obs_precision)


def split_heads(matrix):
    grouped = matrix.reshape(N_LAT, SEQ, HEADS, HEAD_DIM)
    return grouped.transpose(0, 2, 1, 3).reshape(N_LAT * HEADS, SEQ, HEAD_DIM)

def join_heads(stacked):
    grouped = stacked.reshape(N_LAT, HEADS, SEQ, HEAD_DIM)
    return grouped.transpose(0, 2, 1, 3).reshape(TOKENS, D)

def band_scores(query_block, key_block):
    head_scale = 1.0 / math.sqrt(HEAD_DIM)
    return jnp.dot(query_block, key_block.T, preferred_element_type=jnp.float32) * head_scale

def band_log_total(blocks):
    query_block, key_block = blocks
    scores = band_scores(query_block, key_block)
    top_score = lax.optimization_barrier(jnp.max(scores, axis=1))
    return top_score + jnp.log(lax.optimization_barrier(jnp.sum(jnp.exp(scores - top_score[:, None]), axis=1)))

def frozen_weights(query_block, key_block, log_block):
    scores = band_scores(query_block, key_block)
    return jnp.exp(scores - log_block[:, None]).astype(jnp.bfloat16)

def reference(query_states, key_states, silu_slope, w_value, w_out, w_up, w_down, w_obs, obs_cells, obs_weights, obs_count, innovations, obs_precision):
    query_heads = split_heads(query_states)
    key_heads = split_heads(key_states)
    log_heads = lax.map(band_log_total, (query_heads, key_heads))

    def forward_mix(blocks):
        query_block, key_block, log_block, value_block = blocks
        return jnp.dot(frozen_weights(query_block, key_block, log_block), value_block, preferred_element_type=jnp.float32)

    def backward_mix(blocks):
        query_block, key_block, log_block, upward_block = blocks
        return jnp.dot(frozen_weights(query_block, key_block, log_block).T, upward_block, preferred_element_type=jnp.float32)

    def tangent_model(change):
        values = jnp.dot(change.astype(jnp.bfloat16), w_value, preferred_element_type=jnp.float32).astype(jnp.bfloat16)
        mixed_heads = lax.map(forward_mix, (query_heads, key_heads, log_heads, split_heads(values)))
        attended = join_heads(mixed_heads).astype(jnp.bfloat16)
        after_attention = change + jnp.dot(attended, w_out, preferred_element_type=jnp.float32)
        hidden = (jnp.dot(after_attention.astype(jnp.bfloat16), w_up, preferred_element_type=jnp.float32) * silu_slope).astype(jnp.bfloat16)
        return after_attention + jnp.dot(hidden, w_down, preferred_element_type=jnp.float32)

    def adjoint_model(gradient):
        back_hidden = (jnp.dot(gradient.astype(jnp.bfloat16), w_down.T, preferred_element_type=jnp.float32) * silu_slope).astype(jnp.bfloat16)
        middle = gradient + jnp.dot(back_hidden, w_up.T, preferred_element_type=jnp.float32)
        upward = jnp.dot(middle.astype(jnp.bfloat16), w_out.T, preferred_element_type=jnp.float32).astype(jnp.bfloat16)
        spread_heads = lax.map(backward_mix, (query_heads, key_heads, log_heads, split_heads(upward)))
        spread = join_heads(spread_heads).astype(jnp.bfloat16)
        return middle + jnp.dot(spread, w_value.T, preferred_element_type=jnp.float32)
    dest_band = lax.broadcasted_iota(jnp.int32, obs_cells.shape, 3)
    lon_sector = lax.broadcasted_iota(jnp.int32, obs_cells.shape, 1)
    cell_rows = ((dest_band * N_LON + lon_sector) * TOK_DEV + obs_cells).astype(jnp.int32)
    slot_index = lax.broadcasted_iota(jnp.int32, obs_count.shape + (SLOTS,), 3)
    live_slots = (slot_index < obs_count[:, :, :, None]).astype(jnp.float32)
    weight = obs_weights * live_slots[:, :, None, :, :]

    def observe(state_now):
        field_cols = jnp.dot(state_now.astype(jnp.bfloat16), w_obs, preferred_element_type=jnp.float32)
        summed = jnp.zeros((N_LAT, N_LON, N_LAT, SLOTS, CHANNELS), jnp.float32)
        for corner in range(STENCIL):
            summed = summed + weight[:, :, corner, :, :, None] * field_cols[cell_rows[:, :, corner]]
        return summed.transpose(0, 1, 4, 2, 3)

    def observe_adjoint(errors):
        slot_major = errors.transpose(0, 1, 3, 4, 2)
        grad_field = jnp.zeros((TOKENS, CHANNELS), jnp.float32)
        for corner in range(STENCIL):
            weighted = (weight[:, :, corner, :, :, None] * slot_major).reshape(-1, CHANNELS)
            grad_field = grad_field + jax.ops.segment_sum(weighted, cell_rows[:, :, corner].reshape(-1), num_segments=TOKENS)
        return jnp.dot(grad_field.astype(jnp.bfloat16), w_obs.T, preferred_element_type=jnp.float32)
    precision = obs_precision[None, None, :, None, None]
    right_side = adjoint_model(observe_adjoint(precision * innovations))
    solution = jnp.zeros_like(right_side)
    residual = right_side
    direction = right_side
    norm_now = jnp.sum(residual * residual)
    for iteration in range(ITERS):
        applied = direction + adjoint_model(observe_adjoint(precision * observe(tangent_model(direction))))
        step_size = norm_now / jnp.sum(direction * applied)
        solution = solution + step_size * direction
        residual = residual - step_size * applied
        norm_next = jnp.sum(residual * residual)
        direction = residual + norm_next / norm_now * direction
        norm_now = norm_next
    return (solution, residual)
```

```python
import math

import jax
import jax.numpy as jnp
from jax import lax
from jax.experimental import pallas as pl
from jax.experimental.pallas import tpu as pltpu
from jax.sharding import PartitionSpec as P

D = 512
HEADS = 8
HEAD_DIM = 64
FF = 2048
CHANNELS = 128
STENCIL = 4
TOK = 128
SLOTS = 128
N_LAT = 4
GROUP = 16
HALF = GROUP * TOK
SCORE_ROWS = 256
SCORE_SCALE = math.log2(math.e) / math.sqrt(HEAD_DIM)

MESH = pl.DeviceIdType.MESH
F32 = jnp.float32
BF16 = jnp.bfloat16
HIGHEST = lax.Precision.HIGHEST

KEYS, QUERIES, UP0, BACK0, VAL1, ATT1, UP1, BACK1, VAL2, ATT2, UP2, BACK2 = range(12)
STENCILS, ERRORS, STATS, SUMS = 12, 13, 14, 15
N_SUMS = 3
N_SEM = SUMS + 3 * N_SUMS


def mm(a, b):
    return jnp.dot(a, b, preferred_element_type=F32)


def contract(a, b, dim_a, dim_b, precision=None):
    return lax.dot_general(
        a, b, (((dim_a,), (dim_b,)), ((), ())), precision=precision, preferred_element_type=F32
    )


def fold(x):
    rows = jnp.sum(x, axis=0, keepdims=True)
    total = rows[:, 0:128]
    for c in range(128, x.shape[1], 128):
        total = total + rows[:, c : c + 128]
    return total


def kernel(
    query_ref,
    key_ref,
    slope_ref,
    w_value_ref,
    w_out_ref,
    w_up_ref,
    w_down_ref,
    w_obs_ref,
    cells_ref,
    weights_ref,
    count_ref,
    innov_ref,
    prec_ref,
    sol_ref,
    res_ref,
    arrived,
    blocks,
    parts,
    mix,
    stat_mine,
    stat_other,
    scale_ref,
    slope_t,
    st_stage,
    st_arrived,
    er_stage,
    er_arrived,
    sum_stage,
    sum_lat,
    sum_plane,
    sum_pair,
    send,
    recv,
):
    lat = lax.axis_index("lat")
    lon = lax.axis_index("lon")
    x, y, z = lax.div(lon, 8), lax.rem(lax.div(lon, 4), 2), lax.rem(lon, 4)
    i_half = lax.div(x, 2)
    head = lax.rem(x, 2) * 4 + z
    plane_me = x * 4 + z
    slab_me = lon - i_half * GROUP
    pair_lon = lon + 4 - 8 * y

    def plane_lon(t):
        return lax.div(t, 4) * 8 + y * 4 + lax.rem(t, 4)

    def plane_head(t):
        return lax.rem(lax.div(t, 4), 2) * 4 + lax.rem(t, 4)

    def slab_lon(t):
        return i_half * GROUP + t

    def slab_head(t):
        return lax.div(t, 8) * 4 + lax.rem(t, 4)

    def others(me, body):
        def one(k, carry):
            body(lax.rem(me + k, GROUP))
            return carry

        lax.fori_loop(1, GROUP, one, 0)

    def push(src, dst, sem, target):
        pltpu.make_async_remote_copy(
            src_ref=src,
            dst_ref=dst,
            send_sem=send.at[sem],
            recv_sem=recv.at[sem],
            device_id=target,
            device_id_type=MESH,
        ).start()

    def drain(ref, sem):
        pltpu.make_async_copy(ref, ref, sem).wait()

    def scatter_plane(e):
        others(
            plane_me,
            lambda t: push(
                blocks.at[e, plane_head(t)], arrived.at[e, plane_me], e, {"lon": plane_lon(t)}
            ),
        )
        arrived[e, plane_me] = blocks[e, head]

    def scatter_slab(e):
        others(
            slab_me,
            lambda t: push(
                blocks.at[e, slab_head(t)], arrived.at[e, slab_me], e, {"lon": slab_lon(t)}
            ),
        )
        arrived[e, slab_me] = blocks[e, head]

    def return_plane(e, p):
        slot = i_half * HEADS + head
        others(
            plane_me,
            lambda t: push(parts.at[p, t], arrived.at[e, slot], e, {"lon": plane_lon(t)}),
        )
        arrived[e, slot] = parts[p, plane_me]

    def return_slab(e, p):
        slot = y * HEADS + head
        others(
            slab_me,
            lambda t: push(parts.at[p, t], arrived.at[e, slot], e, {"lon": slab_lon(t)}),
        )
        arrived[e, slot] = parts[p, slab_me]

    def wait_group(e):
        drain(arrived.at[e, pl.ds(0, GROUP - 1)], recv.at[e])

    def wide(e):
        return jnp.concatenate([arrived[e, t] for t in range(GROUP)], axis=1)

    def joined(e):
        total = arrived[e, 0:HEADS].astype(F32) + arrived[e, HEADS:GROUP].astype(F32)
        return total.reshape(D, TOK)

    def put_blocks(e, matrix):
        blocks[e] = matrix.reshape(HEADS, HEAD_DIM, TOK)

    def put_parts(p, matrix):
        for t in range(GROUP):
            parts[p, t] = matrix[:, t * TOK : (t + 1) * TOK].astype(BF16)

    def sum_start(n, rows):
        row = lax.broadcasted_iota(jnp.int32, (8, 128), 0)
        tile = jnp.zeros((8, 128), F32)
        for r, values in enumerate(rows):
            tile = jnp.where(row == r, values, tile)
        sum_stage[n, 0] = tile
        sum_lat[n, lat] = tile

        def one(k, carry):
            push(
                sum_stage.at[n, 0],
                sum_lat.at[n, lat],
                SUMS + 3 * n,
                {"lat": lax.rem(lat + k, N_LAT)},
            )
            return carry

        lax.fori_loop(1, N_LAT, one, 0)

    def sum_middle(n):
        drain(sum_lat.at[n, pl.ds(0, N_LAT - 1)], recv.at[SUMS + 3 * n])
        tile = jnp.sum(sum_lat[n], axis=0)
        sum_stage[n, 1] = tile
        sum_plane[n, plane_me] = tile
        others(
            plane_me,
            lambda t: push(
                sum_stage.at[n, 1],
                sum_plane.at[n, plane_me],
                SUMS + 3 * n + 1,
                {"lon": plane_lon(t)},
            ),
        )

    def sum_last(n):
        drain(sum_plane.at[n, pl.ds(0, GROUP - 1)], recv.at[SUMS + 3 * n + 1])
        tile = jnp.sum(sum_plane[n], axis=0)
        sum_stage[n, 2] = tile
        push(sum_stage.at[n, 2], sum_pair.at[n], SUMS + 3 * n + 2, {"lon": pair_lon})

    def sum_end(n, count):
        drain(sum_pair.at[n], recv.at[SUMS + 3 * n + 2])
        tile = sum_stage[n, 2] + sum_pair[n]
        return [jnp.sum(tile[r : r + 1], axis=1, keepdims=True) for r in range(count)]

    barrier = pltpu.get_barrier_semaphore()

    def greet(target):
        pl.semaphore_signal(barrier, inc=1, device_id=target, device_id_type=MESH)

    others(plane_me, lambda t: greet({"lon": plane_lon(t)}))

    def greet_slab(k, carry):
        greet({"lon": i_half * GROUP + lax.div(k, 4) * 8 + (1 - y) * 4 + lax.rem(k, 4)})
        return carry

    lax.fori_loop(0, 8, greet_slab, 0)

    def greet_lat(k, carry):
        greet({"lat": lax.rem(lat + k, N_LAT)})
        return carry

    lax.fori_loop(1, N_LAT, greet_lat, 0)

    put_blocks(KEYS, key_ref[...].astype(F32).T.astype(BF16))
    put_blocks(QUERIES, query_ref[...].astype(F32).T.astype(BF16))
    prec_t = jnp.broadcast_to(prec_ref[...], (128, CHANNELS)).T
    lane = lax.broadcasted_iota(jnp.int32, (STENCIL, SLOTS), 1)
    for d in range(N_LAT):
        st_stage[d, 0:STENCIL] = cells_ref[0, 0, :, d, :].astype(F32)
        st_stage[d, STENCIL : 2 * STENCIL] = jnp.where(
            lane < count_ref[0, 0, d], weights_ref[0, 0, :, d, :], 0.0
        )
        er_stage[d] = (innov_ref[0, 0, :, d, :] * prec_t).astype(BF16)

    pl.semaphore_wait(barrier, GROUP - 1 + 8 + N_LAT - 1)

    def send_lat(k, carry):
        p = lax.rem(lat + k, N_LAT)
        push(st_stage.at[p], st_arrived.at[lat], STENCILS, {"lat": p})
        push(er_stage.at[p], er_arrived.at[lat], ERRORS, {"lat": p})
        return carry

    lax.fori_loop(1, N_LAT, send_lat, 0)
    st_arrived[lat] = st_stage[lat]
    er_arrived[lat] = er_stage[lat]
    scatter_plane(KEYS)
    scatter_slab(QUERIES)

    slope_t[...] = slope_ref[...].astype(F32).T.astype(BF16)

    drain(st_arrived.at[pl.ds(0, N_LAT - 1)], recv.at[STENCILS])
    token = lax.broadcasted_iota(jnp.int32, (TOK, SLOTS), 0).astype(F32)
    columns = []
    for a in range(N_LAT):
        rows = st_arrived[a]
        total = jnp.zeros((TOK, SLOTS), F32)
        for k in range(STENCIL):
            total = total + jnp.where(
                token == rows[k : k + 1], rows[STENCIL + k : STENCIL + k + 1], 0.0
            )
        columns.append(total)
    operator = jnp.concatenate(columns, axis=1)
    gram = contract(operator, operator, 1, 1, HIGHEST)
    drain(er_arrived.at[pl.ds(0, N_LAT - 1)], recv.at[ERRORS])
    errors = jnp.concatenate([er_arrived[a] for a in range(N_LAT)], axis=1).astype(F32)

    def adjoint_out(grad_t, e):
        g = mm(w_obs_ref[...], grad_t.astype(BF16))
        back = (mm(w_down_ref[...], g.astype(BF16)) * slope_t[...].astype(F32)).astype(BF16)
        middle = g + mm(w_up_ref[...], back)
        put_blocks(e, mm(w_out_ref[...], middle.astype(BF16)).astype(BF16))
        scatter_slab(e)
        return middle

    def adjoint_mix(e, p):
        upward = (wide(e).astype(F32) * scale_ref[...]).astype(BF16)
        put_parts(p, mm(upward, mix[...]))

    def adjoint_in(middle, e):
        wait_group(e)
        return (middle + mm(w_value_ref[...], joined(e).astype(BF16))).T

    def tangent_out(v, e):
        values = mm(v.astype(BF16), w_value_ref[...])
        put_blocks(e, values.T.astype(BF16))
        scatter_plane(e)

    def tangent_mix(e, p):
        put_parts(p, contract(wide(e), mix[...], 1, 1) * scale_ref[...])

    def tangent_in(v, attended):
        after = v + mm(attended, w_out_ref[...])
        hidden = (mm(after.astype(BF16), w_up_ref[...]) * slope_ref[...].astype(F32)).astype(BF16)
        y_field = after + mm(hidden, w_down_ref[...])
        field = mm(y_field.astype(BF16), w_obs_ref[...])
        grad_t = contract(field, gram, 0, 0, HIGHEST) * prec_t
        return field, grad_t

    middle = adjoint_out(contract(errors, operator, 1, 1, HIGHEST), UP0)

    wait_group(KEYS)
    wait_group(QUERIES)
    stat_lane = lax.broadcasted_iota(jnp.int32, (SCORE_ROWS, 128), 1)

    def score_rows(c, carry):
        query = jnp.concatenate([arrived[QUERIES, 2 * c], arrived[QUERIES, 2 * c + 1]], axis=1)
        scores = contract(query, wide(KEYS), 0, 0) * SCORE_SCALE
        top = jnp.max(scores, axis=1, keepdims=True)
        raised = jnp.exp2(scores - top)
        total = jnp.sum(raised, axis=1, keepdims=True)
        start = pl.multiple_of(c * SCORE_ROWS, SCORE_ROWS)
        mix[pl.ds(start, SCORE_ROWS), :] = raised.astype(BF16)
        stat = jnp.where(stat_lane == 0, top, total).T
        stat_mine[:, pl.ds(start, SCORE_ROWS)] = stat[0:8]
        return carry

    lax.fori_loop(0, HALF // SCORE_ROWS, score_rows, 0)
    push(stat_mine, stat_other, STATS, {"lon": pair_lon})
    wait_group(UP0)
    drain(stat_other, recv.at[STATS])
    top_mine, top_other = stat_mine[0:1], stat_other[0:1]
    top = jnp.maximum(top_mine, top_other)
    mine = jnp.exp2(top_mine - top)
    scale_ref[...] = mine / (
        stat_mine[1:2] * mine + stat_other[1:2] * jnp.exp2(top_other - top)
    )

    adjoint_mix(UP0, 0)
    return_plane(BACK0, 0)
    r1 = adjoint_in(middle, BACK0)

    tangent_out(r1, VAL1)
    rr1 = fold(r1 * r1)
    wait_group(VAL1)
    tangent_mix(VAL1, 1)
    return_slab(ATT1, 1)
    wait_group(ATT1)
    attended1 = joined(ATT1).T
    field, grad_t = tangent_in(r1, attended1.astype(BF16))
    sum_start(0, [rr1, fold(field * grad_t.T)])
    middle = adjoint_out(grad_t, UP1)
    sum_middle(0)
    wait_group(UP1)
    adjoint_mix(UP1, 2)
    return_plane(BACK1, 2)
    sum_last(0)
    applied = r1 + adjoint_in(middle, BACK1)
    norm1, seen1 = sum_end(0, 2)
    step1 = norm1 / (norm1 + seen1)
    r2 = r1 - step1 * applied

    tangent_out(r2, VAL2)
    sum_start(1, [fold(r2 * r2)])
    wait_group(VAL2)
    sum_middle(1)
    tangent_mix(VAL2, 3)
    return_slab(ATT2, 3)
    sum_last(1)
    wait_group(ATT2)
    (norm2,) = sum_end(1, 1)
    beta = norm2 / norm1
    d2 = r2 + beta * r1
    attended2 = joined(ATT2).T + beta * attended1
    field, grad_t = tangent_in(d2, attended2.astype(BF16))
    sum_start(2, [fold(d2 * d2), fold(field * grad_t.T)])
    middle = adjoint_out(grad_t, UP2)
    sum_middle(2)
    wait_group(UP2)
    adjoint_mix(UP2, 4)
    return_plane(BACK2, 4)
    sum_last(2)
    applied = d2 + adjoint_in(middle, BACK2)
    squared2, seen2 = sum_end(2, 2)
    step2 = norm2 / (squared2 + seen2)
    sol_ref[...] = step1 * r1 + step2 * d2
    res_ref[...] = r2 - step2 * applied

    for e in range(12):
        drain(arrived.at[e, pl.ds(0, GROUP - 1)], send.at[e])
    drain(st_stage.at[pl.ds(0, N_LAT - 1)], send.at[STENCILS])
    drain(er_stage.at[pl.ds(0, N_LAT - 1)], send.at[ERRORS])
    drain(stat_mine, send.at[STATS])
    for n in range(N_SUMS):
        drain(sum_lat.at[n, pl.ds(0, N_LAT - 1)], send.at[SUMS + 3 * n])
        drain(sum_plane.at[n, pl.ds(0, GROUP - 1)], send.at[SUMS + 3 * n + 1])
        drain(sum_pair.at[n], send.at[SUMS + 3 * n + 2])


def per_device(*args):
    args = list(args)
    args[12] = args[12].reshape(1, CHANNELS)
    vmem = pl.BlockSpec(memory_space=pltpu.VMEM)
    in_specs = [vmem] * 13
    in_specs[10] = pl.BlockSpec(memory_space=pltpu.SMEM)
    return pl.pallas_call(
        kernel,
        out_shape=(jax.ShapeDtypeStruct((TOK, D), F32),) * 2,
        in_specs=in_specs,
        out_specs=(vmem, vmem),
        scratch_shapes=[
            pltpu.VMEM((12, GROUP, HEAD_DIM, TOK), BF16),
            pltpu.VMEM((12, HEADS, HEAD_DIM, TOK), BF16),
            pltpu.VMEM((5, GROUP, HEAD_DIM, TOK), BF16),
            pltpu.VMEM((HALF, HALF), BF16),
            pltpu.VMEM((8, HALF), F32),
            pltpu.VMEM((8, HALF), F32),
            pltpu.VMEM((1, HALF), F32),
            pltpu.VMEM((FF, TOK), BF16),
            pltpu.VMEM((N_LAT, 2 * STENCIL, SLOTS), F32),
            pltpu.VMEM((N_LAT, 2 * STENCIL, SLOTS), F32),
            pltpu.VMEM((N_LAT, CHANNELS, SLOTS), BF16),
            pltpu.VMEM((N_LAT, CHANNELS, SLOTS), BF16),
            pltpu.VMEM((N_SUMS, 3, 8, 128), F32),
            pltpu.VMEM((N_SUMS, N_LAT, 8, 128), F32),
            pltpu.VMEM((N_SUMS, GROUP, 8, 128), F32),
            pltpu.VMEM((N_SUMS, 8, 128), F32),
            pltpu.SemaphoreType.DMA((N_SEM,)),
            pltpu.SemaphoreType.DMA((N_SEM,)),
        ],
        compiler_params=pltpu.CompilerParams(
            collective_id=0, has_side_effects=True, vmem_limit_bytes=56 * 1024 * 1024
        ),
    )(*args)


def solution(mesh):
    in_specs = (
        P(("lat", "lon"), None),
        P(("lat", "lon"), None),
        P(("lat", "lon"), None),
        P(),
        P(),
        P(),
        P(),
        P(),
        P("lat", "lon", None, None, None),
        P("lat", "lon", None, None, None),
        P("lat", "lon", None),
        P("lat", "lon", None, None, None),
        P(),
    )
    out_specs = (P(("lat", "lon"), None), P(("lat", "lon"), None))
    return jax.shard_map(
        per_device, mesh=mesh, in_specs=in_specs, out_specs=out_specs, check_vma=False
    )
```

```python
import math

import jax
import jax.numpy as jnp
from jax import lax
from jax.experimental import pallas as pl
from jax.experimental.pallas import tpu as pltpu
from jax.sharding import PartitionSpec as P

D = 512
HEADS = 8
HEAD_DIM = 64
FF = 2048
CHANNELS = 128
STENCIL = 4
TOK = 128
SLOTS = 128
N_LAT = 4
GROUP = 16
HALF = GROUP * TOK
SCORE_SCALE = math.log2(math.e) / math.sqrt(HEAD_DIM)

MESH = pl.DeviceIdType.MESH
F32 = jnp.float32
BF16 = jnp.bfloat16
HIGHEST = lax.Precision.HIGHEST

KEYS, QUERIES, UP0, BACK0, VAL1, ATT1, UP1, BACK1, VAL2, ATT2, UP2, BACK2 = range(12)
N_EXCHANGES = 12
STENCILS, ERRORS, STATS, SUMS = 0, 1, 2, 4
N_SUMS = 3
N_OTHER = SUMS + 3 * N_SUMS


def hops(offset):
    dx, dy, dz = offset
    return dx + dy + min(dz, 4 - dz)


GROUP_OFFSETS = sorted(
    [(dx, dy, dz) for dx in (1, 0) for dy in (1, 0) for dz in (2, 1, 3, 0) if (dx, dy, dz) != (0, 0, 0)],
    key=hops,
    reverse=True,
)


def mm(a, b):
    return jnp.dot(a, b, preferred_element_type=F32)


def contract(a, b, dim_a, dim_b, precision=None):
    return lax.dot_general(
        a, b, (((dim_a,), (dim_b,)), ((), ())), precision=precision, preferred_element_type=F32
    )


def total_of(x):
    return jnp.sum(jnp.sum(x, axis=0, keepdims=True), axis=1, keepdims=True)


def kernel(
    query_hbm,
    key_hbm,
    slope_hbm,
    w_value_hbm,
    w_out_hbm,
    w_up_hbm,
    w_down_hbm,
    w_obs_hbm,
    cells_hbm,
    weights_hbm,
    count_ref,
    innov_hbm,
    prec_hbm,
    sol_ref,
    res_ref,
    query_ref,
    key_ref,
    slope_ref,
    w_value_ref,
    w_out_ref,
    w_up_ref,
    w_down_ref,
    w_obs_ref,
    cells_ref,
    weights_ref,
    innov_ref,
    prec_ref,
    arrived,
    blocks,
    parts,
    half_sum,
    mix,
    stat_mine,
    stat_other,
    scale_ref,
    slope_t,
    st_stage,
    st_arrived,
    er_stage,
    er_arrived,
    sum_stage,
    sum_lat,
    sum_group,
    sum_pair,
    load,
    send,
    recv,
    other_send,
    other_recv,
):
    loads = {}
    for n, (src, dst) in enumerate(
        [
            (key_hbm, key_ref),
            (query_hbm, query_ref),
            (prec_hbm, prec_ref),
            (cells_hbm, cells_ref),
            (weights_hbm, weights_ref),
            (innov_hbm, innov_ref),
            (slope_hbm, slope_ref),
            (w_obs_hbm, w_obs_ref),
            (w_down_hbm, w_down_ref),
            (w_up_hbm, w_up_ref),
            (w_out_hbm, w_out_ref),
            (w_value_hbm, w_value_ref),
        ]
    ):
        loads[id(dst)] = pltpu.make_async_copy(src, dst, load.at[n])
        loads[id(dst)].start()

    lat = lax.axis_index("lat")
    lon = lax.axis_index("lon")
    x, y, z = lax.div(lon, 8), lax.rem(lax.div(lon, 4), 2), lax.rem(lon, 4)
    row = y * 4 + z
    bit_i = lax.rem(x, 2)
    bit_j = 1 - bit_i
    mate_i = x + 1 - 2 * bit_i
    mate_j = lax.rem(x + 5 - 2 * bit_j, 4)
    slot_i = bit_i * 8 + row
    slot_j = bit_j * 8 + row
    rows_by = {
        (dy, dz): (y + dy - 2 * y * dy) * 4 + (lax.rem(z + dz, 4) if dz else z)
        for dy in range(2)
        for dz in range(4)
    }

    def member(by_i, offset):
        dx, dy, dz = offset
        bit = bit_i if by_i else bit_j
        place = x if dx == 0 else (mate_i if by_i else mate_j)
        there = rows_by[dy, dz]
        return (bit + dx - 2 * bit * dx) * 8 + there, place * 8 + there

    def remote(src, dst, send_sem, recv_sem, target):
        pltpu.make_async_remote_copy(
            src_ref=src,
            dst_ref=dst,
            send_sem=send_sem,
            recv_sem=recv_sem,
            device_id=target,
            device_id_type=MESH,
        ).start()

    def push(src, dst, n, target):
        remote(src, dst, other_send.at[n], other_recv.at[n], target)

    def drain(ref, sem):
        pltpu.make_async_copy(ref, ref, sem).wait()

    def scatter(e, by_i, matrix):
        blocks[e] = matrix.reshape(HEADS, HEAD_DIM, TOK)
        me = slot_i if by_i else slot_j
        for offset in GROUP_OFFSETS:
            slot, place = member(by_i, offset)
            remote(
                blocks.at[e, rows_by[offset[1:]]],
                arrived.at[e, me],
                send.at[e],
                recv.at[e, offset[0]],
                {"lon": place},
            )
        arrived[e, me] = blocks[e, row]

    def send_part(e, p, by_i, offset, block):
        me = slot_i if by_i else slot_j
        if offset == (0, 0, 0):
            arrived[e, me] = block
            return
        slot, place = member(by_i, offset)
        parts[p, slot] = block
        remote(
            parts.at[p, slot], arrived.at[e, me], send.at[e], recv.at[e, offset[0]], {"lon": place}
        )

    def wait_near(e):
        drain(arrived.at[e, pl.ds(0, HEADS - 1)], recv.at[e, 0])

    def wait_far(e):
        drain(arrived.at[e, pl.ds(0, HEADS)], recv.at[e, 1])

    def half(e, bit):
        return jnp.concatenate([arrived[e, bit * HEADS + t] for t in range(HEADS)], axis=1)

    def joined(e):
        wait_near(e)
        wait_far(e)
        total = arrived[e, 0:HEADS].astype(F32) + arrived[e, HEADS:GROUP].astype(F32)
        return total.reshape(D, TOK)

    def span(index, size):
        return pl.ds(pl.multiple_of(index * size, size), size)

    def quarters(by_i, one):
        bit = bit_i if by_i else bit_j
        for dx, dy in ((1, 1), (1, 0), (0, 1), (0, 0)):
            quarter = (bit + dx - 2 * bit * dx) * 2 + (y + dy - 2 * y * dy)
            one(quarter, dx, dy)

    lane = lax.broadcasted_iota(jnp.int32, (1, 128), 1)

    def sum_start(n, values):
        tile = jnp.zeros((1, 128), F32)
        for r, value in enumerate(values):
            tile = jnp.where(lane == r, value, tile)
        sum_stage[n, 0] = tile
        sum_lat[n, lat] = tile
        for k in range(1, N_LAT):
            push(
                sum_stage.at[n, 0],
                sum_lat.at[n, lat],
                SUMS + 3 * n,
                {"lat": lax.rem(lat + k, N_LAT)},
            )

    def sum_middle(n):
        drain(sum_lat.at[n, pl.ds(0, N_LAT - 1)], other_recv.at[SUMS + 3 * n])
        tile = jnp.sum(sum_lat[n], axis=0)
        sum_stage[n, 1] = tile
        sum_group[n, slot_i] = tile
        for offset in GROUP_OFFSETS:
            push(
                sum_stage.at[n, 1],
                sum_group.at[n, slot_i],
                SUMS + 3 * n + 1,
                {"lon": member(True, offset)[1]},
            )

    def sum_last(n):
        drain(sum_group.at[n, pl.ds(0, GROUP - 1)], other_recv.at[SUMS + 3 * n + 1])
        sum_stage[n, 2] = jnp.sum(sum_group[n], axis=0)
        push(
            sum_stage.at[n, 2],
            sum_pair.at[n],
            SUMS + 3 * n + 2,
            {"lon": mate_j * 8 + row},
        )

    def sum_end(n, count):
        drain(sum_pair.at[n], other_recv.at[SUMS + 3 * n + 2])
        tile = sum_stage[n, 2] + sum_pair[n]
        return [
            jnp.sum(jnp.where(lane == r, tile, 0.0), axis=1, keepdims=True) for r in range(count)
        ]

    barrier = pltpu.get_barrier_semaphore()

    def greet(target):
        pl.semaphore_signal(barrier, inc=1, device_id=target, device_id_type=MESH)

    for offset in GROUP_OFFSETS:
        greet({"lon": member(True, offset)[1]})
    for offset in GROUP_OFFSETS:
        if offset[0] == 1:
            greet({"lon": member(False, offset)[1]})
    for k in range(1, N_LAT):
        greet({"lat": lax.rem(lat + k, N_LAT)})

    loads[id(key_ref)].wait()
    keys_t = key_ref[...].astype(F32).T.astype(BF16)
    loads[id(query_ref)].wait()
    queries_t = query_ref[...].astype(F32).T.astype(BF16)
    loads[id(prec_ref)].wait()
    prec_t = jnp.broadcast_to(prec_ref[...], (128, CHANNELS)).T
    loads[id(cells_ref)].wait()
    loads[id(weights_ref)].wait()
    loads[id(innov_ref)].wait()
    slot_lane = lax.broadcasted_iota(jnp.int32, (STENCIL, SLOTS), 1)
    for d in range(N_LAT):
        st_stage[d, 0:STENCIL] = cells_ref[0, 0, :, d, :].astype(F32)
        st_stage[d, STENCIL : 2 * STENCIL] = jnp.where(
            slot_lane < count_ref[0, 0, d], weights_ref[0, 0, :, d, :], 0.0
        )
        er_stage[d] = (innov_ref[0, 0, :, d, :] * prec_t).astype(BF16)

    pl.semaphore_wait(barrier, GROUP - 1 + HEADS + N_LAT - 1)

    scatter(KEYS, False, keys_t)
    for k in range(1, N_LAT):
        p = lax.rem(lat + k, N_LAT)
        push(st_stage.at[p], st_arrived.at[lat], STENCILS, {"lat": p})
        push(er_stage.at[p], er_arrived.at[lat], ERRORS, {"lat": p})
    st_arrived[lat] = st_stage[lat]
    er_arrived[lat] = er_stage[lat]
    scatter(QUERIES, True, queries_t)

    loads[id(slope_ref)].wait()
    slope_t[...] = slope_ref[...].astype(F32).T.astype(BF16)

    drain(st_arrived.at[pl.ds(0, N_LAT - 1)], other_recv.at[STENCILS])
    token = lax.broadcasted_iota(jnp.int32, (TOK, SLOTS), 0).astype(F32)
    columns = []
    for a in range(N_LAT):
        rows = st_arrived[a]
        total = jnp.zeros((TOK, SLOTS), F32)
        for k in range(STENCIL):
            total = total + jnp.where(
                token == rows[k : k + 1], rows[STENCIL + k : STENCIL + k + 1], 0.0
            )
        columns.append(total)
    operator = jnp.concatenate(columns, axis=1)
    gram = contract(operator, operator, 1, 1, HIGHEST)
    drain(er_arrived.at[pl.ds(0, N_LAT - 1)], other_recv.at[ERRORS])
    errors = jnp.concatenate([er_arrived[a] for a in range(N_LAT)], axis=1).astype(F32)
    for ref in (w_obs_ref, w_down_ref, w_up_ref, w_out_ref, w_value_ref):
        loads[id(ref)].wait()

    def adjoint_out(grad_t, e):
        g = mm(w_obs_ref[...], grad_t.astype(BF16))
        back = (mm(w_down_ref[...], g.astype(BF16)) * slope_t[...].astype(F32)).astype(BF16)
        middle = g + mm(w_up_ref[...], back)
        scatter(e, True, mm(w_out_ref[...], middle.astype(BF16)).astype(BF16))
        return middle

    def adjoint_mix(e, back, p):
        wait_near(e)
        upward = (half(e, bit_i).astype(F32) * scale_ref[:, span(bit_i, HALF // 2)]).astype(BF16)
        half_sum[...] = mm(upward, mix[span(bit_i, HALF // 2), :])
        wait_far(e)
        rest = (half(e, bit_j).astype(F32) * scale_ref[:, span(bit_j, HALF // 2)]).astype(BF16)

        def one(quarter, dx, dy):
            cols = span(quarter, HALF // 4)
            half_sum[:, cols] += mm(rest, mix[span(bit_j, HALF // 2), cols])
            for dz in (2, 1, 3, 0):
                piece = half_sum[:, span(quarter * 4 + lax.rem(z + dz, 4), TOK)]
                send_part(back, p, False, (dx, dy, dz), piece.astype(BF16))

        quarters(False, one)

    def adjoint_in(middle, e):
        return (middle + mm(w_value_ref[...], joined(e).astype(BF16))).T

    def tangent_out(v, e):
        scatter(e, False, mm(v.astype(BF16), w_value_ref[...]).T.astype(BF16))

    def tangent_mix(e, back, p):
        wait_near(e)
        half_sum[...] = contract(half(e, bit_j), mix[:, span(bit_j, HALF // 2)], 1, 1)
        wait_far(e)
        rest = half(e, bit_i)

        def one(quarter, dx, dy):
            cols = span(quarter, HALF // 4)
            out = half_sum[:, cols] + contract(rest, mix[cols, span(bit_i, HALF // 2)], 1, 1)
            half_sum[:, cols] = out * scale_ref[:, cols]
            for dz in (2, 1, 3, 0):
                piece = half_sum[:, span(quarter * 4 + lax.rem(z + dz, 4), TOK)]
                send_part(back, p, True, (dx, dy, dz), piece.astype(BF16))

        quarters(True, one)

    def tangent_in(v, attended):
        after = v + mm(attended, w_out_ref[...])
        hidden = (mm(after.astype(BF16), w_up_ref[...]) * slope_ref[...].astype(F32)).astype(BF16)
        y_field = after + mm(hidden, w_down_ref[...])
        field = mm(y_field.astype(BF16), w_obs_ref[...])
        grad_t = contract(field, gram, 0, 0, HIGHEST) * prec_t
        return field, grad_t

    middle = adjoint_out(contract(errors, operator, 1, 1, HIGHEST), UP0)

    wait_near(KEYS)
    wait_far(KEYS)
    stat_lane = lax.broadcasted_iota(jnp.int32, (TOK, 128), 1)
    keys = jnp.concatenate([arrived[KEYS, t] for t in range(GROUP)], axis=1)
    keys = jnp.concatenate([keys, keys], axis=0)

    def score_rows(slot):
        scaled = arrived[QUERIES, slot].astype(F32) * SCORE_SCALE
        high = scaled.astype(BF16)
        low = (scaled - high.astype(F32)).astype(BF16)
        scores = contract(jnp.concatenate([high, low], axis=0), keys, 0, 0)
        top = jnp.max(scores, axis=1, keepdims=True)
        raised = jnp.exp2(scores - top)
        total = jnp.sum(raised, axis=1, keepdims=True)
        mix[span(slot, TOK), :] = raised.astype(BF16)
        stat = jnp.where(stat_lane == 0, top, total).T
        stat_mine[:, span(slot, TOK)] = stat[0:8]

    pair = {"lon": mate_i * 8 + row}

    def score_half(bit, sem):
        for t in range(HEADS):
            score_rows(bit * HEADS + t)
        place = span(bit, HALF // 2)
        push(stat_mine.at[:, place], stat_other.at[:, place], sem, pair)

    def set_scale(bit, sem):
        place = span(bit, HALF // 2)
        drain(stat_other.at[:, pl.ds(0, HALF // 2)], other_recv.at[sem])
        top_mine, top_other = stat_mine[0:1, place], stat_other[0:1, place]
        top = jnp.maximum(top_mine, top_other)
        mine = jnp.exp2(top_mine - top)
        scale_ref[:, place] = mine / (
            stat_mine[1:2, place] * mine + stat_other[1:2, place] * jnp.exp2(top_other - top)
        )

    wait_near(QUERIES)
    wait_far(QUERIES)
    score_half(0, STATS)
    score_half(1, STATS + 1)
    set_scale(0, STATS)
    set_scale(1, STATS + 1)

    adjoint_mix(UP0, BACK0, 0)
    r1 = adjoint_in(middle, BACK0)

    tangent_out(r1, VAL1)
    rr1 = total_of(r1 * r1)
    tangent_mix(VAL1, ATT1, 1)
    attended1 = joined(ATT1).T
    field, grad_t = tangent_in(r1, attended1.astype(BF16))
    sum_start(0, [rr1, total_of(field * grad_t.T)])
    middle = adjoint_out(grad_t, UP1)
    sum_middle(0)
    adjoint_mix(UP1, BACK1, 2)
    sum_last(0)
    applied = r1 + adjoint_in(middle, BACK1)
    norm1, seen1 = sum_end(0, 2)
    step1 = norm1 / (norm1 + seen1)
    r2 = r1 - step1 * applied

    tangent_out(r2, VAL2)
    sum_start(1, [total_of(r2 * r2)])
    sum_middle(1)
    tangent_mix(VAL2, ATT2, 3)
    sum_last(1)
    attended2 = joined(ATT2).T
    (norm2,) = sum_end(1, 1)
    beta = norm2 / norm1
    d2 = r2 + beta * r1
    attended2 = attended2 + beta * attended1
    field, grad_t = tangent_in(d2, attended2.astype(BF16))
    sum_start(2, [total_of(d2 * d2), total_of(field * grad_t.T)])
    middle = adjoint_out(grad_t, UP2)
    sum_middle(2)
    adjoint_mix(UP2, BACK2, 4)
    sum_last(2)
    applied = d2 + adjoint_in(middle, BACK2)
    squared2, seen2 = sum_end(2, 2)
    step2 = norm2 / (squared2 + seen2)
    sol_ref[...] = step1 * r1 + step2 * d2
    res_ref[...] = r2 - step2 * applied

    for e in range(N_EXCHANGES):
        drain(arrived.at[e, pl.ds(0, GROUP - 1)], send.at[e])
    drain(st_stage.at[pl.ds(0, N_LAT - 1)], other_send.at[STENCILS])
    drain(er_stage.at[pl.ds(0, N_LAT - 1)], other_send.at[ERRORS])
    for k in range(2):
        drain(stat_mine.at[:, pl.ds(0, HALF // 2)], other_send.at[STATS + k])
    for n in range(N_SUMS):
        drain(sum_lat.at[n, pl.ds(0, N_LAT - 1)], other_send.at[SUMS + 3 * n])
        drain(sum_group.at[n, pl.ds(0, GROUP - 1)], other_send.at[SUMS + 3 * n + 1])
        drain(sum_pair.at[n], other_send.at[SUMS + 3 * n + 2])


def per_device(*args):
    args = list(args)
    args[12] = args[12].reshape(1, CHANNELS)
    hbm = pl.BlockSpec(memory_space=pl.ANY)
    vmem = pl.BlockSpec(memory_space=pltpu.VMEM)
    in_specs = [hbm] * 13
    in_specs[10] = pl.BlockSpec(memory_space=pltpu.SMEM)
    return pl.pallas_call(
        kernel,
        out_shape=(jax.ShapeDtypeStruct((TOK, D), F32),) * 2,
        in_specs=in_specs,
        out_specs=(vmem, vmem),
        scratch_shapes=[
            *[pltpu.VMEM(a.shape, a.dtype) for n, a in enumerate(args) if n != 10],
            pltpu.VMEM((N_EXCHANGES, GROUP, HEAD_DIM, TOK), BF16),
            pltpu.VMEM((N_EXCHANGES, HEADS, HEAD_DIM, TOK), BF16),
            pltpu.VMEM((5, GROUP, HEAD_DIM, TOK), BF16),
            pltpu.VMEM((HEAD_DIM, HALF), F32),
            pltpu.VMEM((HALF, HALF), BF16),
            pltpu.VMEM((8, HALF), F32),
            pltpu.VMEM((8, HALF), F32),
            pltpu.VMEM((1, HALF), F32),
            pltpu.VMEM((FF, TOK), BF16),
            pltpu.VMEM((N_LAT, 2 * STENCIL, SLOTS), F32),
            pltpu.VMEM((N_LAT, 2 * STENCIL, SLOTS), F32),
            pltpu.VMEM((N_LAT, CHANNELS, SLOTS), BF16),
            pltpu.VMEM((N_LAT, CHANNELS, SLOTS), BF16),
            pltpu.VMEM((N_SUMS, 3, 1, 128), F32),
            pltpu.VMEM((N_SUMS, N_LAT, 1, 128), F32),
            pltpu.VMEM((N_SUMS, GROUP, 1, 128), F32),
            pltpu.VMEM((N_SUMS, 1, 128), F32),
            pltpu.SemaphoreType.DMA((12,)),
            pltpu.SemaphoreType.DMA((N_EXCHANGES,)),
            pltpu.SemaphoreType.DMA((N_EXCHANGES, 2)),
            pltpu.SemaphoreType.DMA((N_OTHER,)),
            pltpu.SemaphoreType.DMA((N_OTHER,)),
        ],
        compiler_params=pltpu.CompilerParams(
            collective_id=0, has_side_effects=True, vmem_limit_bytes=56 * 1024 * 1024
        ),
    )(*args)


def solution(mesh):
    in_specs = (
        P(("lat", "lon"), None),
        P(("lat", "lon"), None),
        P(("lat", "lon"), None),
        P(),
        P(),
        P(),
        P(),
        P(),
        P("lat", "lon", None, None, None),
        P("lat", "lon", None, None, None),
        P("lat", "lon", None),
        P("lat", "lon", None, None, None),
        P(),
    )
    out_specs = (P(("lat", "lon"), None), P(("lat", "lon"), None))
    return jax.shard_map(
        per_device, mesh=mesh, in_specs=in_specs, out_specs=out_specs, check_vma=False
    )
```

```python
import math

import jax
import jax.numpy as jnp
from jax import lax
from jax.experimental import pallas as pl
from jax.experimental.pallas import tpu as pltpu
from jax.sharding import PartitionSpec as P

D = 512
HEADS = 8
HEAD_DIM = 64
FF = 2048
CHANNELS = 128
STENCIL = 4
TOK = 128
SLOTS = 128
N_LAT = 4
GROUP = 16
HALF = GROUP * TOK
SCORE_SCALE = math.log2(math.e) / math.sqrt(HEAD_DIM)

MESH = pl.DeviceIdType.MESH
F32 = jnp.float32
BF16 = jnp.bfloat16
HIGHEST = lax.Precision.HIGHEST

KEYS, QUERIES, UP0, BACK0, VAL1, ATT1, UP1, BACK1, VAL2, ATT2, UP2, BACK2 = range(12)
N_EXCHANGES = 12
STENCILS, ERRORS, STATS, SUMS = 0, 1, 2, 4
N_SUMS = 3
N_OTHER = SUMS + 3 * N_SUMS


def hops(offset):
    dx, dy, dz = offset
    return dx + dy + min(dz, 4 - dz)


GROUP_OFFSETS = sorted(
    [(dx, dy, dz) for dx in (1, 0) for dy in (1, 0) for dz in (2, 1, 3, 0) if (dx, dy, dz) != (0, 0, 0)],
    key=hops,
    reverse=True,
)


def mm(a, b):
    return jnp.dot(a, b, preferred_element_type=F32)


def contract(a, b, dim_a, dim_b, precision=None):
    return lax.dot_general(
        a, b, (((dim_a,), (dim_b,)), ((), ())), precision=precision, preferred_element_type=F32
    )


def total_of(x):
    return jnp.sum(jnp.sum(x, axis=0, keepdims=True), axis=1, keepdims=True)


def kernel(
    query_hbm,
    key_hbm,
    slope_hbm,
    w_value_hbm,
    w_out_hbm,
    w_up_hbm,
    w_down_hbm,
    w_obs_hbm,
    cells_hbm,
    weights_hbm,
    count_ref,
    innov_hbm,
    prec_hbm,
    sol_ref,
    res_ref,
    query_ref,
    key_ref,
    slope_ref,
    w_value_ref,
    w_out_ref,
    w_up_ref,
    w_down_ref,
    w_obs_ref,
    cells_ref,
    weights_ref,
    innov_ref,
    prec_ref,
    arrived,
    blocks,
    parts,
    half_sum,
    mix,
    stat_mine,
    stat_other,
    scale_ref,
    slope_t,
    w_do,
    w_oo,
    w_ou,
    w_value_t,
    w_vv,
    st_stage,
    st_arrived,
    er_stage,
    er_arrived,
    sum_stage,
    sum_lat,
    sum_group,
    sum_pair,
    load,
    send,
    recv,
    other_send,
    other_recv,
):
    loads = {}

    def start_loads(pairs):
        for src, dst in pairs:
            loads[id(dst)] = pltpu.make_async_copy(src, dst, load.at[len(loads)])
            loads[id(dst)].start()

    start_loads([(key_hbm, key_ref), (query_hbm, query_ref)])

    lat = lax.axis_index("lat")
    lon = lax.axis_index("lon")
    x, y, z = lax.div(lon, 8), lax.rem(lax.div(lon, 4), 2), lax.rem(lon, 4)
    row = y * 4 + z
    bit_i = lax.rem(x, 2)
    bit_j = 1 - bit_i
    mate_i = x + 1 - 2 * bit_i
    mate_j = lax.rem(x + 5 - 2 * bit_j, 4)
    slot_i = y * 8 + bit_i * 4 + z
    slot_j = y * 8 + bit_j * 4 + z
    near, far = y, 1 - y
    rows_by = {
        (dy, dz): (y + dy - 2 * y * dy) * 4 + (lax.rem(z + dz, 4) if dz else z)
        for dy in range(2)
        for dz in range(4)
    }

    def member(by_i, offset):
        dx, dy, dz = offset
        bit = bit_i if by_i else bit_j
        place = x if dx == 0 else (mate_i if by_i else mate_j)
        there = rows_by[dy, dz]
        slot = (y + dy - 2 * y * dy) * 8 + (bit + dx - 2 * bit * dx) * 4 + lax.rem(z + dz, 4)
        return slot, place * 8 + there

    def remote(src, dst, send_sem, recv_sem, target):
        pltpu.make_async_remote_copy(
            src_ref=src,
            dst_ref=dst,
            send_sem=send_sem,
            recv_sem=recv_sem,
            device_id=target,
            device_id_type=MESH,
        ).start()

    def push(src, dst, n, target):
        remote(src, dst, other_send.at[n], other_recv.at[n], target)

    def drain(ref, sem):
        pltpu.make_async_copy(ref, ref, sem).wait()

    def scatter(e, by_i, matrix):
        blocks[e] = matrix.reshape(HEADS, HEAD_DIM, TOK)
        me = slot_i if by_i else slot_j
        for offset in sorted(GROUP_OFFSETS, key=lambda o: o[1]):
            slot, place = member(by_i, offset)
            remote(
                blocks.at[e, rows_by[offset[1:]]],
                arrived.at[e, me],
                send.at[e],
                recv.at[e, offset[1]],
                {"lon": place},
            )
        arrived[e, me] = blocks[e, row]

    def send_part(e, p, by_i, offset, block):
        me = slot_i if by_i else slot_j
        if offset == (0, 0, 0):
            arrived[e, me] = block
            return
        slot, place = member(by_i, offset)
        parts[p, slot] = block
        remote(
            parts.at[p, slot], arrived.at[e, me], send.at[e], recv.at[e, offset[1]], {"lon": place}
        )

    def wait_near(e):
        drain(arrived.at[e, pl.ds(0, HEADS - 1)], recv.at[e, 0])

    def wait_far(e):
        drain(arrived.at[e, pl.ds(0, HEADS)], recv.at[e, 1])

    def half(e, bit):
        return jnp.concatenate([arrived[e, bit * HEADS + t] for t in range(HEADS)], axis=1)

    def joined(e):
        wait_near(e)
        wait_far(e)
        quarter = [arrived[e, 4 * q : 4 * q + 4].astype(F32) for q in range(4)]
        total = jnp.concatenate([quarter[0] + quarter[1], quarter[2] + quarter[3]], axis=0)
        return total.reshape(D, TOK).astype(BF16)

    def span(index, size):
        return pl.ds(pl.multiple_of(index * size, size), size)

    def quarters(by_i, one):
        bit = bit_i if by_i else bit_j
        for dx, dy in ((1, 1), (0, 1), (1, 0), (0, 0)):
            quarter = (y + dy - 2 * y * dy) * 2 + (bit + dx - 2 * bit * dx)
            one(quarter, dx, dy)

    lane = lax.broadcasted_iota(jnp.int32, (1, 128), 1)

    def sum_start(n, values):
        tile = jnp.zeros((1, 128), F32)
        for r, value in enumerate(values):
            tile = jnp.where(lane == r, value, tile)
        sum_stage[n, 0] = tile
        sum_lat[n, lat] = tile
        for k in range(1, N_LAT):
            push(
                sum_stage.at[n, 0],
                sum_lat.at[n, lat],
                SUMS + 3 * n,
                {"lat": lax.rem(lat + k, N_LAT)},
            )

    def sum_middle(n):
        drain(sum_lat.at[n, pl.ds(0, N_LAT - 1)], other_recv.at[SUMS + 3 * n])
        tile = jnp.sum(sum_lat[n], axis=0)
        sum_stage[n, 1] = tile
        sum_group[n, slot_i] = tile
        for offset in GROUP_OFFSETS:
            push(
                sum_stage.at[n, 1],
                sum_group.at[n, slot_i],
                SUMS + 3 * n + 1,
                {"lon": member(True, offset)[1]},
            )

    def sum_last(n):
        drain(sum_group.at[n, pl.ds(0, GROUP - 1)], other_recv.at[SUMS + 3 * n + 1])
        sum_stage[n, 2] = jnp.sum(sum_group[n], axis=0)
        push(
            sum_stage.at[n, 2],
            sum_pair.at[n],
            SUMS + 3 * n + 2,
            {"lon": mate_j * 8 + row},
        )

    def sum_end(n, count):
        drain(sum_pair.at[n], other_recv.at[SUMS + 3 * n + 2])
        tile = sum_stage[n, 2] + sum_pair[n]
        return [
            jnp.sum(jnp.where(lane == r, tile, 0.0), axis=1, keepdims=True) for r in range(count)
        ]

    barrier = pltpu.get_barrier_semaphore()

    def greet(target):
        pl.semaphore_signal(barrier, inc=1, device_id=target, device_id_type=MESH)

    for offset in GROUP_OFFSETS:
        greet({"lon": member(True, offset)[1]})
    for offset in GROUP_OFFSETS:
        if offset[0] == 1:
            greet({"lon": member(False, offset)[1]})
    for k in range(1, N_LAT):
        greet({"lat": lax.rem(lat + k, N_LAT)})

    start_loads(
        [
            (prec_hbm, prec_ref),
            (cells_hbm, cells_ref),
            (weights_hbm, weights_ref),
            (innov_hbm, innov_ref),
            (slope_hbm, slope_ref),
            (w_obs_hbm, w_obs_ref),
            (w_down_hbm, w_down_ref),
            (w_out_hbm, w_out_ref),
            (w_up_hbm, w_up_ref),
            (w_value_hbm, w_value_ref),
        ]
    )
    loads[id(key_ref)].wait()
    keys_t = key_ref[...].astype(F32).T.astype(BF16)
    loads[id(query_ref)].wait()
    queries_t = query_ref[...].astype(F32).T.astype(BF16)
    loads[id(prec_ref)].wait()
    prec_t = jnp.broadcast_to(prec_ref[...], (128, CHANNELS)).T
    loads[id(cells_ref)].wait()
    loads[id(weights_ref)].wait()
    loads[id(innov_ref)].wait()
    slot_lane = lax.broadcasted_iota(jnp.int32, (STENCIL, SLOTS), 1)
    for d in range(N_LAT):
        st_stage[d, 0:STENCIL] = cells_ref[0, 0, :, d, :].astype(F32)
        st_stage[d, STENCIL : 2 * STENCIL] = jnp.where(
            slot_lane < count_ref[0, 0, d], weights_ref[0, 0, :, d, :], 0.0
        )
        er_stage[d] = (innov_ref[0, 0, :, d, :] * prec_t).astype(BF16)
    pl.semaphore_wait(barrier, GROUP - 1 + HEADS + N_LAT - 1)
    for k in range(1, N_LAT):
        p = lax.rem(lat + k, N_LAT)
        push(st_stage.at[p], st_arrived.at[lat], STENCILS, {"lat": p})
        push(er_stage.at[p], er_arrived.at[lat], ERRORS, {"lat": p})
    st_arrived[lat] = st_stage[lat]
    er_arrived[lat] = er_stage[lat]
    scatter(KEYS, False, keys_t)
    scatter(QUERIES, True, queries_t)

    loads[id(slope_ref)].wait()
    slope_t[...] = slope_ref[...].astype(F32).T.astype(BF16)
    for ref in (w_obs_ref, w_down_ref, w_out_ref, w_up_ref, w_value_ref):
        loads[id(ref)].wait()

    drain(st_arrived.at[pl.ds(0, N_LAT - 1)], other_recv.at[STENCILS])
    token = lax.broadcasted_iota(jnp.int32, (TOK, SLOTS), 0).astype(F32)
    columns = []
    for a in range(N_LAT):
        rows = st_arrived[a]
        total = jnp.zeros((TOK, SLOTS), F32)
        for k in range(STENCIL):
            total = total + jnp.where(
                token == rows[k : k + 1], rows[STENCIL + k : STENCIL + k + 1], 0.0
            )
        columns.append(total)
    operator = jnp.concatenate(columns, axis=1)
    drain(er_arrived.at[pl.ds(0, N_LAT - 1)], other_recv.at[ERRORS])
    errors = jnp.concatenate([er_arrived[a] for a in range(N_LAT)], axis=1).astype(F32)

    def adjoint_out(grad, e):
        back = (mm(w_do[...], grad) * slope_t[...].astype(F32)).astype(BF16)
        scatter(e, True, (mm(w_ou[...], back) + mm(w_oo[...], grad)).astype(BF16))
        return back

    def adjoint_middle(grad, back):
        middle = mm(w_obs_ref[...], grad) + mm(w_up_ref[...], back)
        return middle, values_of(middle)

    def values_of(middle):
        high = middle.astype(BF16)
        low = (middle - high.astype(F32)).astype(BF16)
        return mm(w_value_t[...], high) + mm(w_value_t[...], low)

    def adjoint_mix(e, back, p):
        wait_near(e)
        upward = (half(e, near).astype(F32) * scale_ref[:, span(near, HALF // 2)]).astype(BF16)
        half_sum[...] = mm(upward, mix[span(near, HALF // 2), :])
        wait_far(e)
        if p == 0:
            set_scale(far, STATS + 1)
        rest = (half(e, far).astype(F32) * scale_ref[:, span(far, HALF // 2)]).astype(BF16)

        def one(quarter, dx, dy):
            cols = span(quarter, HALF // 4)
            half_sum[:, cols] += mm(rest, mix[span(far, HALF // 2), cols])
            for dz in (2, 1, 3, 0):
                piece = half_sum[:, span(quarter * 4 + lax.rem(z + dz, 4), TOK)]
                send_part(back, p, False, (dx, dy, dz), piece.astype(BF16))

        quarters(False, one)

    def tangent_mix(e, back, p, between=None):
        wait_near(e)
        half_sum[...] = contract(half(e, near), mix[:, span(near, HALF // 2)], 1, 1)
        if between is not None:
            between(1)
        wait_far(e)
        rest = half(e, far)

        def one(quarter, dx, dy):
            cols = span(quarter, HALF // 4)
            out = half_sum[:, cols] + contract(rest, mix[cols, span(far, HALF // 2)], 1, 1)
            half_sum[:, cols] = out * scale_ref[:, cols]
            for dz in (2, 1, 3, 0):
                piece = half_sum[:, span(quarter * 4 + lax.rem(z + dz, 4), TOK)]
                send_part(back, p, True, (dx, dy, dz), piece.astype(BF16))

        quarters(True, one)

    def tangent_start(v):
        v_in = v.astype(BF16)
        return mm(v_in, w_up_ref[...]), mm(v_in, w_obs_ref[...])

    def tangent_in(started, attended):
        hidden_v, field_v = started
        hidden = hidden_v + mm(attended, w_ou[...])
        hidden = (hidden * slope_ref[...].astype(F32)).astype(BF16)
        field = field_v + mm(attended, w_oo[...]) + mm(hidden, w_do[...])
        grad_t = contract(field, gram, 0, 0, HIGHEST) * prec_t
        return field, grad_t

    grad = contract(errors, operator, 1, 1, HIGHEST).astype(BF16)
    start = mm(w_obs_ref[...], grad)
    back = (mm(w_down_ref[...], start.astype(BF16)) * slope_t[...].astype(F32)).astype(BF16)
    middle = start + mm(w_up_ref[...], back)
    scatter(UP0, True, mm(w_out_ref[...], middle.astype(BF16)).astype(BF16))
    gram = contract(operator, operator, 1, 1, HIGHEST)

    wait_near(KEYS)
    wait_far(KEYS)
    stat_lane = lax.broadcasted_iota(jnp.int32, (TOK, 128), 1)
    keys = jnp.concatenate([arrived[KEYS, t] for t in range(GROUP)], axis=1)
    keys = jnp.concatenate([keys, keys], axis=0)

    def score_rows(slot):
        scaled = arrived[QUERIES, slot].astype(F32) * SCORE_SCALE
        high = scaled.astype(BF16)
        low = (scaled - high.astype(F32)).astype(BF16)
        scores = contract(jnp.concatenate([high, low], axis=0), keys, 0, 0)
        top = jnp.max(scores, axis=1, keepdims=True)
        raised = jnp.exp2(scores - top)
        total = jnp.sum(raised, axis=1, keepdims=True)
        mix[span(slot, TOK), :] = raised.astype(BF16)
        stat = jnp.where(stat_lane == 0, top, total).T
        stat_mine[:, span(slot, TOK)] = stat[0:8]

    pair = {"lon": mate_i * 8 + row}

    def score_half(bit, sem):
        for t in range(HEADS):
            score_rows(bit * HEADS + t)
        place = span(bit, HALF // 2)
        push(stat_mine.at[:, place], stat_other.at[:, place], sem, pair)

    def set_scale(bit, sem):
        place = span(bit, HALF // 2)
        drain(stat_other.at[:, pl.ds(0, HALF // 2)], other_recv.at[sem])
        top_mine, top_other = stat_mine[0:1, place], stat_other[0:1, place]
        top = jnp.maximum(top_mine, top_other)
        mine = jnp.exp2(top_mine - top)
        scale_ref[:, place] = mine / (
            stat_mine[1:2, place] * mine + stat_other[1:2, place] * jnp.exp2(top_other - top)
        )

    wait_near(QUERIES)
    score_half(near, STATS)
    wait_far(QUERIES)
    score_half(far, STATS + 1)
    set_scale(near, STATS)

    adjoint_mix(UP0, BACK0, 0)

    w_value_t[...] = w_value_ref[...].astype(F32).T.astype(BF16)
    w_vv[...] = mm(w_value_t[...], w_value_ref[...]).astype(BF16)
    middle_values = values_of(middle)
    w_do[...] = mm(w_down_ref[...], w_obs_ref[...]).astype(BF16)
    w_oo[...] = mm(w_out_ref[...], w_obs_ref[...]).astype(BF16)
    w_ou[...] = mm(w_out_ref[...], w_up_ref[...]).astype(BF16)
    spread = joined(BACK0)

    values1 = middle_values + mm(w_vv[...], spread)
    scatter(VAL1, False, values1.astype(BF16))
    r1 = (middle + mm(w_value_ref[...], spread)).T
    rr1 = total_of(r1 * r1)
    tangent_mix(VAL1, ATT1, 1)
    started = tangent_start(r1)
    attended1 = joined(ATT1).astype(F32).T
    field, grad_t = tangent_in(started, attended1.astype(BF16))
    grad = grad_t.astype(BF16)
    sum_start(0, [rr1, total_of(field * grad_t.T)])
    back = adjoint_out(grad, UP1)
    sum_middle(0)
    middle, middle_values = adjoint_middle(grad, back)
    adjoint_mix(UP1, BACK1, 2)
    sum_last(0)
    norm1, seen1 = sum_end(0, 2)
    step1 = norm1 / (norm1 + seen1)
    values2 = values1 - step1 * (values1 + middle_values)
    spread = joined(BACK1)

    values2 = values2 - step1 * mm(w_vv[...], spread)
    scatter(VAL2, False, values2.astype(BF16))
    applied = r1 + (middle + mm(w_value_ref[...], spread)).T
    r2 = r1 - step1 * applied
    sum_start(1, [total_of(r2 * r2)])
    tangent_mix(VAL2, ATT2, 3, sum_middle)
    sum_last(1)
    (norm2,) = sum_end(1, 1)
    beta = norm2 / norm1
    d2 = r2 + beta * r1
    started = tangent_start(d2)
    attended2 = joined(ATT2).astype(F32).T + beta * attended1
    field, grad_t = tangent_in(started, attended2.astype(BF16))
    grad = grad_t.astype(BF16)
    sum_start(2, [total_of(d2 * d2), total_of(field * grad_t.T)])
    back = adjoint_out(grad, UP2)
    sum_middle(2)
    middle = mm(w_obs_ref[...], grad) + mm(w_up_ref[...], back)
    base = (d2 + middle.T)
    adjoint_mix(UP2, BACK2, 4)
    sum_last(2)
    squared2, seen2 = sum_end(2, 2)
    step2 = norm2 / (squared2 + seen2)
    sol_ref[...] = step1 * r1 + step2 * d2
    base = r2 - step2 * base
    spread = joined(BACK2)
    res_ref[...] = base - step2 * mm(w_value_ref[...], spread).T

    for e in range(N_EXCHANGES):
        drain(arrived.at[e, pl.ds(0, GROUP - 1)], send.at[e])
    drain(st_stage.at[pl.ds(0, N_LAT - 1)], other_send.at[STENCILS])
    drain(er_stage.at[pl.ds(0, N_LAT - 1)], other_send.at[ERRORS])
    for k in range(2):
        drain(stat_mine.at[:, pl.ds(0, HALF // 2)], other_send.at[STATS + k])
    for n in range(N_SUMS):
        drain(sum_lat.at[n, pl.ds(0, N_LAT - 1)], other_send.at[SUMS + 3 * n])
        drain(sum_group.at[n, pl.ds(0, GROUP - 1)], other_send.at[SUMS + 3 * n + 1])
        drain(sum_pair.at[n], other_send.at[SUMS + 3 * n + 2])


def per_device(*args):
    args = list(args)
    args[12] = args[12].reshape(1, CHANNELS)
    hbm = pl.BlockSpec(memory_space=pl.ANY)
    vmem = pl.BlockSpec(memory_space=pltpu.VMEM)
    in_specs = [hbm] * 13
    in_specs[10] = pl.BlockSpec(memory_space=pltpu.SMEM)
    return pl.pallas_call(
        kernel,
        out_shape=(pltpu.VMEM((TOK, D), F32),) * 2,
        in_specs=in_specs,
        out_specs=(vmem, vmem),
        scratch_shapes=[
            *[pltpu.VMEM(a.shape, a.dtype) for n, a in enumerate(args) if n != 10],
            pltpu.VMEM((N_EXCHANGES, GROUP, HEAD_DIM, TOK), BF16),
            pltpu.VMEM((N_EXCHANGES, HEADS, HEAD_DIM, TOK), BF16),
            pltpu.VMEM((5, GROUP, HEAD_DIM, TOK), BF16),
            pltpu.VMEM((HEAD_DIM, HALF), F32),
            pltpu.VMEM((HALF, HALF), BF16),
            pltpu.VMEM((8, HALF), F32),
            pltpu.VMEM((8, HALF), F32),
            pltpu.VMEM((1, HALF), F32),
            pltpu.VMEM((FF, TOK), BF16),
            pltpu.VMEM((FF, CHANNELS), BF16),
            pltpu.VMEM((D, CHANNELS), BF16),
            pltpu.VMEM((D, FF), BF16),
            pltpu.VMEM((D, D), BF16),
            pltpu.VMEM((D, D), BF16),
            pltpu.VMEM((N_LAT, 2 * STENCIL, SLOTS), F32),
            pltpu.VMEM((N_LAT, 2 * STENCIL, SLOTS), F32),
            pltpu.VMEM((N_LAT, CHANNELS, SLOTS), BF16),
            pltpu.VMEM((N_LAT, CHANNELS, SLOTS), BF16),
            pltpu.VMEM((N_SUMS, 3, 1, 128), F32),
            pltpu.VMEM((N_SUMS, N_LAT, 1, 128), F32),
            pltpu.VMEM((N_SUMS, GROUP, 1, 128), F32),
            pltpu.VMEM((N_SUMS, 1, 128), F32),
            pltpu.SemaphoreType.DMA((12,)),
            pltpu.SemaphoreType.DMA((N_EXCHANGES,)),
            pltpu.SemaphoreType.DMA((N_EXCHANGES, 2)),
            pltpu.SemaphoreType.DMA((N_OTHER,)),
            pltpu.SemaphoreType.DMA((N_OTHER,)),
        ],
        compiler_params=pltpu.CompilerParams(
            collective_id=0, has_side_effects=True, vmem_limit_bytes=56 * 1024 * 1024
        ),
    )(*args)


def solution(mesh):
    in_specs = (
        P(("lat", "lon"), None),
        P(("lat", "lon"), None),
        P(("lat", "lon"), None),
        P(),
        P(),
        P(),
        P(),
        P(),
        P("lat", "lon", None, None, None),
        P("lat", "lon", None, None, None),
        P("lat", "lon", None),
        P("lat", "lon", None, None, None),
        P(),
    )
    out_specs = (P(("lat", "lon"), None), P(("lat", "lon"), None))
    return jax.shard_map(
        per_device, mesh=mesh, in_specs=in_specs, out_specs=out_specs, check_vma=False
    )
```

```python
import math

import jax
import jax.numpy as jnp
from jax import lax
from jax.experimental import pallas as pl
from jax.experimental.pallas import tpu as pltpu
from jax.sharding import PartitionSpec as P

D = 512
HEADS = 8
HEAD_DIM = 64
FF = 2048
CHANNELS = 128
STENCIL = 4
TOK = 128
SLOTS = 128
N_LAT = 4
GROUP = 16
HALF = GROUP * TOK
SCORE_SCALE = math.log2(math.e) / math.sqrt(HEAD_DIM)

MESH = pl.DeviceIdType.MESH
F32 = jnp.float32
BF16 = jnp.bfloat16
HIGHEST = lax.Precision.HIGHEST

KEYS, QUERIES, UP0, BACK0, VAL1, ATT1, UP1, BACK1, VAL2, ATT2, UP2, BACK2 = range(12)
N_EXCHANGES = 12
STENCILS, ERRORS, STATS, SUMS = 0, 1, 2, 4
N_SUMS = 2
N_OTHER = SUMS + 3 * N_SUMS


def hops(offset):
    dx, dy, dz = offset
    return dx + dy + min(dz, 4 - dz)


GROUP_OFFSETS = sorted(
    [(dx, dy, dz) for dx in (1, 0) for dy in (1, 0) for dz in (2, 1, 3, 0) if (dx, dy, dz) != (0, 0, 0)],
    key=hops,
    reverse=True,
)


def mm(a, b):
    return jnp.dot(a, b, preferred_element_type=F32)


def contract(a, b, dim_a, dim_b, precision=None):
    return lax.dot_general(
        a, b, (((dim_a,), (dim_b,)), ((), ())), precision=precision, preferred_element_type=F32
    )


def total_of(x):
    return jnp.sum(jnp.sum(x, axis=0, keepdims=True), axis=1, keepdims=True)


def kernel(
    query_hbm,
    key_hbm,
    slope_hbm,
    w_value_hbm,
    w_out_hbm,
    w_up_hbm,
    w_down_hbm,
    w_obs_hbm,
    cells_hbm,
    weights_hbm,
    count_ref,
    innov_hbm,
    prec_hbm,
    sol_ref,
    res_ref,
    query_ref,
    key_ref,
    slope_ref,
    w_value_ref,
    w_out_ref,
    w_up_ref,
    w_down_ref,
    w_obs_ref,
    cells_ref,
    weights_ref,
    innov_ref,
    prec_ref,
    arrived,
    blocks,
    parts,
    half_sum,
    mix,
    mix_t,
    stat_mine,
    stat_other,
    scale_ref,
    slope_t,
    w_do,
    w_oo,
    w_ou,
    w_value_t,
    w_vv,
    st_stage,
    st_arrived,
    er_stage,
    er_arrived,
    sum_stage,
    sum_lat,
    sum_group,
    sum_pair,
    load,
    send,
    recv,
    other_send,
    other_recv,
):
    loads = {}

    def start_loads(pairs):
        for src, dst in pairs:
            loads[id(dst)] = pltpu.make_async_copy(src, dst, load.at[len(loads)])
            loads[id(dst)].start()

    start_loads([(key_hbm, key_ref), (query_hbm, query_ref)])

    lat = lax.axis_index("lat")
    lon = lax.axis_index("lon")
    x, y, z = lax.div(lon, 8), lax.rem(lax.div(lon, 4), 2), lax.rem(lon, 4)
    row = y * 4 + z
    bit_i = lax.rem(x, 2)
    bit_j = 1 - bit_i
    mate_i = x + 1 - 2 * bit_i
    mate_j = lax.rem(x + 5 - 2 * bit_j, 4)
    slot_i = y * 8 + bit_i * 4 + z
    slot_j = y * 8 + bit_j * 4 + z
    near, far = y, 1 - y
    rows_by = {
        (dy, dz): (y + dy - 2 * y * dy) * 4 + (lax.rem(z + dz, 4) if dz else z)
        for dy in range(2)
        for dz in range(4)
    }

    def member(by_i, offset):
        dx, dy, dz = offset
        bit = bit_i if by_i else bit_j
        place = x if dx == 0 else (mate_i if by_i else mate_j)
        there = rows_by[dy, dz]
        slot = (y + dy - 2 * y * dy) * 8 + (bit + dx - 2 * bit * dx) * 4 + lax.rem(z + dz, 4)
        return slot, place * 8 + there

    def remote(src, dst, send_sem, recv_sem, target):
        pltpu.make_async_remote_copy(
            src_ref=src,
            dst_ref=dst,
            send_sem=send_sem,
            recv_sem=recv_sem,
            device_id=target,
            device_id_type=MESH,
        ).start()

    def push(src, dst, n, target):
        remote(src, dst, other_send.at[n], other_recv.at[n], target)

    def drain(ref, sem):
        pltpu.make_async_copy(ref, ref, sem).wait()

    def scatter(e, by_i, matrix):
        blocks[e] = matrix.reshape(HEADS, HEAD_DIM, TOK)
        me = slot_i if by_i else slot_j
        for offset in sorted(GROUP_OFFSETS, key=lambda o: o[1]):
            slot, place = member(by_i, offset)
            remote(
                blocks.at[e, rows_by[offset[1:]]],
                arrived.at[e, me],
                send.at[e],
                recv.at[e, offset[1]],
                {"lon": place},
            )
        arrived[e, me] = blocks[e, row]

    def send_part(e, p, by_i, offset, block):
        me = slot_i if by_i else slot_j
        if offset == (0, 0, 0):
            arrived[e, me] = block
            return
        slot, place = member(by_i, offset)
        parts[p, slot] = block
        remote(
            parts.at[p, slot], arrived.at[e, me], send.at[e], recv.at[e, offset[1]], {"lon": place}
        )

    def wait_near(e):
        drain(arrived.at[e, pl.ds(0, HEADS - 1)], recv.at[e, 0])

    def wait_far(e):
        drain(arrived.at[e, pl.ds(0, HEADS)], recv.at[e, 1])

    def half(e, bit):
        return jnp.concatenate([arrived[e, bit * HEADS + t] for t in range(HEADS)], axis=1)

    def joined(e):
        wait_near(e)
        wait_far(e)
        quarter = [arrived[e, 4 * q : 4 * q + 4].astype(F32) for q in range(4)]
        total = jnp.concatenate([quarter[0] + quarter[1], quarter[2] + quarter[3]], axis=0)
        return total.reshape(D, TOK).astype(BF16)

    def span(index, size):
        return pl.ds(pl.multiple_of(index * size, size), size)

    def quarters(by_i, one):
        bit = bit_i if by_i else bit_j
        for dx, dy in ((1, 1), (0, 1), (1, 0), (0, 0)):
            quarter = (y + dy - 2 * y * dy) * 2 + (bit + dx - 2 * bit * dx)
            one(quarter, dx, dy)

    lane = lax.broadcasted_iota(jnp.int32, (1, 128), 1)

    def sum_start(n, values):
        tile = jnp.zeros((1, 128), F32)
        for r, value in enumerate(values):
            tile = jnp.where(lane == r, value, tile)
        sum_stage[n, 0] = tile
        sum_lat[n, lat] = tile
        for k in range(1, N_LAT):
            push(
                sum_stage.at[n, 0],
                sum_lat.at[n, lat],
                SUMS + 3 * n,
                {"lat": lax.rem(lat + k, N_LAT)},
            )

    def sum_middle(n):
        drain(sum_lat.at[n, pl.ds(0, N_LAT - 1)], other_recv.at[SUMS + 3 * n])
        tile = jnp.sum(sum_lat[n], axis=0)
        sum_stage[n, 1] = tile
        sum_group[n, slot_i] = tile
        for offset in GROUP_OFFSETS:
            push(
                sum_stage.at[n, 1],
                sum_group.at[n, slot_i],
                SUMS + 3 * n + 1,
                {"lon": member(True, offset)[1]},
            )

    def sum_last(n):
        drain(sum_group.at[n, pl.ds(0, GROUP - 1)], other_recv.at[SUMS + 3 * n + 1])
        sum_stage[n, 2] = jnp.sum(sum_group[n], axis=0)
        push(
            sum_stage.at[n, 2],
            sum_pair.at[n],
            SUMS + 3 * n + 2,
            {"lon": mate_j * 8 + row},
        )

    def sum_end(n, count):
        drain(sum_pair.at[n], other_recv.at[SUMS + 3 * n + 2])
        tile = sum_stage[n, 2] + sum_pair[n]
        return [
            jnp.sum(jnp.where(lane == r, tile, 0.0), axis=1, keepdims=True) for r in range(count)
        ]

    barrier = pltpu.get_barrier_semaphore()

    def greet(target):
        pl.semaphore_signal(barrier, inc=1, device_id=target, device_id_type=MESH)

    for offset in GROUP_OFFSETS:
        greet({"lon": member(True, offset)[1]})
    for offset in GROUP_OFFSETS:
        if offset[0] == 1:
            greet({"lon": member(False, offset)[1]})
    for k in range(1, N_LAT):
        greet({"lat": lax.rem(lat + k, N_LAT)})

    start_loads(
        [
            (prec_hbm, prec_ref),
            (cells_hbm, cells_ref),
            (weights_hbm, weights_ref),
            (innov_hbm, innov_ref),
            (slope_hbm, slope_ref),
            (w_obs_hbm, w_obs_ref),
            (w_down_hbm, w_down_ref),
            (w_out_hbm, w_out_ref),
            (w_up_hbm, w_up_ref),
            (w_value_hbm, w_value_ref),
        ]
    )
    loads[id(key_ref)].wait()
    keys_t = key_ref[...].astype(F32).T.astype(BF16)
    loads[id(query_ref)].wait()
    queries_t = query_ref[...].astype(F32).T.astype(BF16)
    loads[id(prec_ref)].wait()
    prec_t = jnp.broadcast_to(prec_ref[...], (128, CHANNELS)).T
    loads[id(cells_ref)].wait()
    loads[id(weights_ref)].wait()
    loads[id(innov_ref)].wait()
    slot_lane = lax.broadcasted_iota(jnp.int32, (STENCIL, SLOTS), 1)
    for d in range(N_LAT):
        st_stage[d, 0:STENCIL] = cells_ref[0, 0, :, d, :].astype(F32)
        st_stage[d, STENCIL : 2 * STENCIL] = jnp.where(
            slot_lane < count_ref[0, 0, d], weights_ref[0, 0, :, d, :], 0.0
        )
        er_stage[d] = (innov_ref[0, 0, :, d, :] * prec_t).astype(BF16)
    pl.semaphore_wait(barrier, GROUP - 1 + HEADS + N_LAT - 1)
    for k in range(1, N_LAT):
        p = lax.rem(lat + k, N_LAT)
        push(st_stage.at[p], st_arrived.at[lat], STENCILS, {"lat": p})
        push(er_stage.at[p], er_arrived.at[lat], ERRORS, {"lat": p})
    st_arrived[lat] = st_stage[lat]
    er_arrived[lat] = er_stage[lat]
    scatter(KEYS, False, keys_t)
    scatter(QUERIES, True, queries_t)

    loads[id(slope_ref)].wait()
    slope_t[...] = slope_ref[...].astype(F32).T.astype(BF16)
    for ref in (w_obs_ref, w_down_ref, w_out_ref, w_up_ref, w_value_ref):
        loads[id(ref)].wait()

    drain(st_arrived.at[pl.ds(0, N_LAT - 1)], other_recv.at[STENCILS])
    token = lax.broadcasted_iota(jnp.int32, (TOK, SLOTS), 0).astype(F32)
    columns = []
    for a in range(N_LAT):
        rows = st_arrived[a]
        total = jnp.zeros((TOK, SLOTS), F32)
        for k in range(STENCIL):
            total = total + jnp.where(
                token == rows[k : k + 1], rows[STENCIL + k : STENCIL + k + 1], 0.0
            )
        columns.append(total)
    operator = jnp.concatenate(columns, axis=1)
    drain(er_arrived.at[pl.ds(0, N_LAT - 1)], other_recv.at[ERRORS])
    errors = jnp.concatenate([er_arrived[a] for a in range(N_LAT)], axis=1).astype(F32)

    def adjoint_out(grad, e):
        back = (mm(w_do[...], grad) * slope_t[...].astype(F32)).astype(BF16)
        scatter(e, True, (mm(w_ou[...], back) + mm(w_oo[...], grad)).astype(BF16))
        return back

    def adjoint_middle(grad, back):
        middle = mm(w_obs_ref[...], grad) + mm(w_up_ref[...], back)
        return middle, values_of(middle)

    def values_of(middle):
        high = middle.astype(BF16)
        low = (middle - high.astype(F32)).astype(BF16)
        return mm(w_value_t[...], high) + mm(w_value_t[...], low)

    def adjoint_mix(e, back, p):
        wait_near(e)
        upward = (half(e, near).astype(F32) * scale_ref[:, span(near, HALF // 2)]).astype(BF16)
        half_sum[...] = mm(upward, mix[span(near, HALF // 2), :])
        wait_far(e)
        if p == 0:
            set_scale(far, STATS + 1)
        rest = (half(e, far).astype(F32) * scale_ref[:, span(far, HALF // 2)]).astype(BF16)

        def one(quarter, dx, dy):
            cols = span(quarter, HALF // 4)
            half_sum[:, cols] += mm(rest, mix[span(far, HALF // 2), cols])
            for dz in (2, 1, 3, 0):
                piece = half_sum[:, span(quarter * 4 + lax.rem(z + dz, 4), TOK)]
                send_part(back, p, False, (dx, dy, dz), piece.astype(BF16))

        quarters(False, one)

    def tangent_mix(e, back, p):
        wait_near(e)
        half_sum[...] = mm(half(e, near), mix_t[span(near, HALF // 2), :])
        wait_far(e)
        rest = half(e, far)

        def one(quarter, dx, dy):
            cols = span(quarter, HALF // 4)
            out = half_sum[:, cols] + mm(rest, mix_t[span(far, HALF // 2), cols])
            half_sum[:, cols] = out * scale_ref[:, cols]
            for dz in (2, 1, 3, 0):
                piece = half_sum[:, span(quarter * 4 + lax.rem(z + dz, 4), TOK)]
                send_part(back, p, True, (dx, dy, dz), piece.astype(BF16))

        quarters(True, one)

    def tangent_start(v):
        v_in = v.astype(BF16)
        return mm(v_in, w_up_ref[...]), mm(v_in, w_obs_ref[...])

    def tangent_in(started, attended):
        hidden_v, field_v = started
        hidden = hidden_v + mm(attended, w_ou[...])
        hidden = (hidden * slope_ref[...].astype(F32)).astype(BF16)
        field = field_v + mm(attended, w_oo[...]) + mm(hidden, w_do[...])
        grad_t = contract(field, gram, 0, 0, HIGHEST) * prec_t
        return field, grad_t

    grad = contract(errors, operator, 1, 1, HIGHEST).astype(BF16)
    start = mm(w_obs_ref[...], grad)
    back = (mm(w_down_ref[...], start.astype(BF16)) * slope_t[...].astype(F32)).astype(BF16)
    middle = start + mm(w_up_ref[...], back)
    scatter(UP0, True, mm(w_out_ref[...], middle.astype(BF16)).astype(BF16))
    gram = contract(operator, operator, 1, 1, HIGHEST)

    wait_near(KEYS)
    wait_far(KEYS)
    stat_lane = lax.broadcasted_iota(jnp.int32, (TOK, 128), 1)
    keys = jnp.concatenate([arrived[KEYS, t] for t in range(GROUP)], axis=1)
    keys = jnp.concatenate([keys, keys], axis=0)

    def query_of(slot):
        scaled = arrived[QUERIES, slot].astype(F32) * SCORE_SCALE
        high = scaled.astype(BF16)
        low = (scaled - high.astype(F32)).astype(BF16)
        return jnp.concatenate([high, low], axis=0)

    def keys_of(slot):
        return jnp.concatenate([arrived[KEYS, slot], arrived[KEYS, slot]], axis=0)

    def score_rows(slot):
        scores = contract(query_of(slot), keys, 0, 0)
        top = jnp.max(scores, axis=1, keepdims=True)
        raised = jnp.exp2(scores - top)
        total = jnp.sum(raised, axis=1, keepdims=True)
        mix[span(slot, TOK), :] = raised.astype(BF16)
        stat = jnp.where(stat_lane == 0, top, total).T
        stat_mine[:, span(slot, TOK)] = stat[0:8]

    pair = {"lon": mate_i * 8 + row}

    def score_half(bit, sem):
        for t in range(HEADS):
            score_rows(bit * HEADS + t)
        place = span(bit, HALF // 2)
        push(stat_mine.at[:, place], stat_other.at[:, place], sem, pair)

    def set_scale(bit, sem):
        place = span(bit, HALF // 2)
        drain(stat_other.at[:, pl.ds(0, HALF // 2)], other_recv.at[sem])
        top_mine, top_other = stat_mine[0:1, place], stat_other[0:1, place]
        top = jnp.maximum(top_mine, top_other)
        mine = jnp.exp2(top_mine - top)
        scale_ref[:, place] = mine / (
            stat_mine[1:2, place] * mine + stat_other[1:2, place] * jnp.exp2(top_other - top)
        )

    wait_near(QUERIES)
    score_half(near, STATS)
    wait_far(QUERIES)
    score_half(far, STATS + 1)
    set_scale(near, STATS)

    adjoint_mix(UP0, BACK0, 0)

    w_value_t[...] = w_value_ref[...].astype(F32).T.astype(BF16)
    w_vv[...] = mm(w_value_t[...], w_value_ref[...]).astype(BF16)
    middle_values = values_of(middle)
    w_do[...] = mm(w_down_ref[...], w_obs_ref[...]).astype(BF16)
    w_oo[...] = mm(w_out_ref[...], w_obs_ref[...]).astype(BF16)
    w_ou[...] = mm(w_out_ref[...], w_up_ref[...]).astype(BF16)
    spread = joined(BACK0)

    values1 = middle_values + mm(w_vv[...], spread)
    scatter(VAL1, False, values1.astype(BF16))
    r1 = (middle + mm(w_value_ref[...], spread)).T
    queries = jnp.concatenate([query_of(t) for t in range(GROUP)], axis=1)
    rr1 = total_of(r1 * r1)
    for t in range(GROUP):
        mix_t[t * TOK : (t + 1) * TOK, :] = jnp.exp2(
            contract(keys_of(t), queries, 0, 0) - stat_mine[0:1, :]
        ).astype(BF16)
    tangent_mix(VAL1, ATT1, 1)
    started = tangent_start(r1)
    attended = joined(ATT1).astype(F32).T.astype(BF16)
    field, grad_t = tangent_in(started, attended)
    grad = grad_t.astype(BF16)
    grad_1 = grad_t.T
    sum_start(0, [rr1, total_of(field * grad_1)])
    back = adjoint_out(grad, UP1)
    sum_middle(0)
    middle, middle_values = adjoint_middle(grad, back)
    adjoint_mix(UP1, BACK1, 2)
    sum_last(0)
    norm1, seen1 = sum_end(0, 2)
    step1 = norm1 / (norm1 + seen1)
    values2 = values1 - step1 * (values1 + middle_values)
    spread = joined(BACK1)

    values2 = values2 - step1 * mm(w_vv[...], spread)
    scatter(VAL2, False, values2.astype(BF16))
    applied = r1 + (middle + mm(w_value_ref[...], spread)).T
    r2 = r1 - step1 * applied
    tangent_mix(VAL2, ATT2, 3)
    started = tangent_start(r2)
    norms = [total_of(r2 * r2), total_of(r2 * r1)]
    attended = joined(ATT2).astype(F32).T.astype(BF16)
    field, grad_t = tangent_in(started, attended)
    grad = grad_t.astype(BF16)
    sum_start(1, norms + [total_of(field * grad_t.T), total_of(field * grad_1)])
    back = adjoint_out(grad, UP2)
    sum_middle(1)
    partial = r2 + (mm(w_obs_ref[...], grad) + mm(w_up_ref[...], back)).T
    adjoint_mix(UP2, BACK2, 4)
    sum_last(1)
    norm2, cross2, seen2, cross_seen2 = sum_end(1, 4)
    beta = norm2 / norm1
    step2 = norm2 / (
        norm2 + seen2 + 2.0 * beta * (cross2 + cross_seen2) + beta * beta * (norm1 + seen1)
    )
    sol_ref[...] = step1 * r1 + step2 * (r2 + beta * r1)
    partial = r2 - step2 * (partial + beta * applied)
    spread = joined(BACK2)
    res_ref[...] = partial - step2 * mm(w_value_ref[...], spread).T

    for e in range(N_EXCHANGES):
        drain(arrived.at[e, pl.ds(0, GROUP - 1)], send.at[e])
    drain(st_stage.at[pl.ds(0, N_LAT - 1)], other_send.at[STENCILS])
    drain(er_stage.at[pl.ds(0, N_LAT - 1)], other_send.at[ERRORS])
    for k in range(2):
        drain(stat_mine.at[:, pl.ds(0, HALF // 2)], other_send.at[STATS + k])
    for n in range(N_SUMS):
        drain(sum_lat.at[n, pl.ds(0, N_LAT - 1)], other_send.at[SUMS + 3 * n])
        drain(sum_group.at[n, pl.ds(0, GROUP - 1)], other_send.at[SUMS + 3 * n + 1])
        drain(sum_pair.at[n], other_send.at[SUMS + 3 * n + 2])


def per_device(*args):
    args = list(args)
    args[12] = args[12].reshape(1, CHANNELS)
    hbm = pl.BlockSpec(memory_space=pl.ANY)
    vmem = pl.BlockSpec(memory_space=pltpu.VMEM)
    in_specs = [hbm] * 13
    in_specs[10] = pl.BlockSpec(memory_space=pltpu.SMEM)
    return pl.pallas_call(
        kernel,
        out_shape=(pltpu.VMEM((TOK, D), F32),) * 2,
        in_specs=in_specs,
        out_specs=(vmem, vmem),
        scratch_shapes=[
            *[pltpu.VMEM(a.shape, a.dtype) for n, a in enumerate(args) if n != 10],
            pltpu.VMEM((N_EXCHANGES, GROUP, HEAD_DIM, TOK), BF16),
            pltpu.VMEM((N_EXCHANGES, HEADS, HEAD_DIM, TOK), BF16),
            pltpu.VMEM((5, GROUP, HEAD_DIM, TOK), BF16),
            pltpu.VMEM((HEAD_DIM, HALF), F32),
            pltpu.VMEM((HALF, HALF), BF16),
            pltpu.VMEM((HALF, HALF), BF16),
            pltpu.VMEM((8, HALF), F32),
            pltpu.VMEM((8, HALF), F32),
            pltpu.VMEM((1, HALF), F32),
            pltpu.VMEM((FF, TOK), BF16),
            pltpu.VMEM((FF, CHANNELS), BF16),
            pltpu.VMEM((D, CHANNELS), BF16),
            pltpu.VMEM((D, FF), BF16),
            pltpu.VMEM((D, D), BF16),
            pltpu.VMEM((D, D), BF16),
            pltpu.VMEM((N_LAT, 2 * STENCIL, SLOTS), F32),
            pltpu.VMEM((N_LAT, 2 * STENCIL, SLOTS), F32),
            pltpu.VMEM((N_LAT, CHANNELS, SLOTS), BF16),
            pltpu.VMEM((N_LAT, CHANNELS, SLOTS), BF16),
            pltpu.VMEM((N_SUMS, 3, 1, 128), F32),
            pltpu.VMEM((N_SUMS, N_LAT, 1, 128), F32),
            pltpu.VMEM((N_SUMS, GROUP, 1, 128), F32),
            pltpu.VMEM((N_SUMS, 1, 128), F32),
            pltpu.SemaphoreType.DMA((12,)),
            pltpu.SemaphoreType.DMA((N_EXCHANGES,)),
            pltpu.SemaphoreType.DMA((N_EXCHANGES, 2)),
            pltpu.SemaphoreType.DMA((N_OTHER,)),
            pltpu.SemaphoreType.DMA((N_OTHER,)),
        ],
        compiler_params=pltpu.CompilerParams(
            collective_id=0, has_side_effects=True, vmem_limit_bytes=56 * 1024 * 1024
        ),
    )(*args)


def solution(mesh):
    in_specs = (
        P(("lat", "lon"), None),
        P(("lat", "lon"), None),
        P(("lat", "lon"), None),
        P(),
        P(),
        P(),
        P(),
        P(),
        P("lat", "lon", None, None, None),
        P("lat", "lon", None, None, None),
        P("lat", "lon", None),
        P("lat", "lon", None, None, None),
        P(),
    )
    out_specs = (P(("lat", "lon"), None), P(("lat", "lon"), None))
    return jax.shard_map(
        per_device, mesh=mesh, in_specs=in_specs, out_specs=out_specs, check_vma=False
    )
```

```python
import math

import jax
import jax.numpy as jnp
from jax import lax
from jax.experimental import pallas as pl
from jax.experimental.pallas import tpu as pltpu
from jax.sharding import PartitionSpec as P

D = 512
HEADS = 8
HEAD_DIM = 64
FF = 2048
CHANNELS = 128
STENCIL = 4
TOK = 128
SLOTS = 128
N_LAT = 4
GROUP = 16
HALF = GROUP * TOK
SCORE_SCALE = math.log2(math.e) / math.sqrt(HEAD_DIM)

MESH = pl.DeviceIdType.MESH
F32 = jnp.float32
BF16 = jnp.bfloat16
HIGHEST = lax.Precision.HIGHEST

KEYS, QUERIES, UP0, BACK0, VAL1, ATT1, UP1, BACK1, VAL2, ATT2, UP2, BACK2 = range(12)
N_EXCHANGES = 12
STENCILS, ERRORS, STATS, SUMS = 0, 1, 2, 4
N_SUMS = 2
N_OTHER = SUMS + 3 * N_SUMS


def hops(offset):
    dx, dy, dz = offset
    return dx + dy + min(dz, 4 - dz)


GROUP_OFFSETS = sorted(
    [(dx, dy, dz) for dx in (1, 0) for dy in (1, 0) for dz in (2, 1, 3, 0) if (dx, dy, dz) != (0, 0, 0)],
    key=hops,
    reverse=True,
)


def mm(a, b):
    return jnp.dot(a, b, preferred_element_type=F32)


def contract(a, b, dim_a, dim_b, precision=None):
    return lax.dot_general(
        a, b, (((dim_a,), (dim_b,)), ((), ())), precision=precision, preferred_element_type=F32
    )


def total_of(x):
    return jnp.sum(jnp.sum(x, axis=0, keepdims=True), axis=1, keepdims=True)


def kernel(
    query_hbm,
    key_hbm,
    slope_hbm,
    w_value_hbm,
    w_out_hbm,
    w_up_hbm,
    w_down_hbm,
    w_obs_hbm,
    cells_hbm,
    weights_hbm,
    count_ref,
    innov_hbm,
    prec_hbm,
    sol_ref,
    res_ref,
    query_ref,
    key_ref,
    slope_ref,
    w_value_ref,
    w_out_ref,
    w_up_ref,
    w_down_ref,
    w_obs_ref,
    cells_ref,
    weights_ref,
    innov_ref,
    prec_ref,
    arrived,
    blocks,
    parts,
    half_sum,
    mix,
    mix_t,
    stat_mine,
    stat_other,
    scale_ref,
    slope_t,
    w_do,
    w_oo,
    w_ou,
    w_value_t,
    w_vv,
    st_stage,
    st_arrived,
    er_stage,
    er_arrived,
    sum_stage,
    sum_lat,
    sum_group,
    sum_pair,
    load,
    send,
    recv,
    other_send,
    other_recv,
):
    loads = {}

    def start_loads(pairs):
        for src, dst in pairs:
            loads[id(dst)] = pltpu.make_async_copy(src, dst, load.at[len(loads)])
            loads[id(dst)].start()

    start_loads([(key_hbm, key_ref), (query_hbm, query_ref)])

    lat = lax.axis_index("lat")
    lon = lax.axis_index("lon")
    x, y, z = lax.div(lon, 8), lax.rem(lax.div(lon, 4), 2), lax.rem(lon, 4)
    row = y * 4 + z
    bit_i = lax.rem(x, 2)
    bit_j = 1 - bit_i
    mate_i = x + 1 - 2 * bit_i
    mate_j = lax.rem(x + 5 - 2 * bit_j, 4)
    slot_i = y * 8 + bit_i * 4 + z
    slot_j = y * 8 + bit_j * 4 + z
    near, far = y, 1 - y
    rows_by = {
        (dy, dz): (y + dy - 2 * y * dy) * 4 + (lax.rem(z + dz, 4) if dz else z)
        for dy in range(2)
        for dz in range(4)
    }

    def member(by_i, offset):
        dx, dy, dz = offset
        bit = bit_i if by_i else bit_j
        place = x if dx == 0 else (mate_i if by_i else mate_j)
        there = rows_by[dy, dz]
        slot = (y + dy - 2 * y * dy) * 8 + (bit + dx - 2 * bit * dx) * 4 + lax.rem(z + dz, 4)
        return slot, place * 8 + there

    def remote(src, dst, send_sem, recv_sem, target):
        pltpu.make_async_remote_copy(
            src_ref=src,
            dst_ref=dst,
            send_sem=send_sem,
            recv_sem=recv_sem,
            device_id=target,
            device_id_type=MESH,
        ).start()

    def push(src, dst, n, target):
        remote(src, dst, other_send.at[n], other_recv.at[n], target)

    def drain(ref, sem):
        pltpu.make_async_copy(ref, ref, sem).wait()

    def scatter(e, by_i, matrix):
        blocks[e] = matrix.reshape(HEADS, HEAD_DIM, TOK)
        me = slot_i if by_i else slot_j
        for offset in sorted(GROUP_OFFSETS, key=lambda o: o[1]):
            slot, place = member(by_i, offset)
            remote(
                blocks.at[e, rows_by[offset[1:]]],
                arrived.at[e, me],
                send.at[e],
                recv.at[e, offset[1]],
                {"lon": place},
            )
        arrived[e, me] = blocks[e, row]

    def send_part(e, p, by_i, offset, block):
        me = slot_i if by_i else slot_j
        if offset == (0, 0, 0):
            arrived[e, me] = block
            return
        slot, place = member(by_i, offset)
        parts[p, slot] = block
        remote(
            parts.at[p, slot], arrived.at[e, me], send.at[e], recv.at[e, offset[1]], {"lon": place}
        )

    def wait_near(e):
        drain(arrived.at[e, pl.ds(0, HEADS - 1)], recv.at[e, 0])

    def wait_far(e):
        drain(arrived.at[e, pl.ds(0, HEADS)], recv.at[e, 1])

    def half(e, bit):
        return jnp.concatenate([arrived[e, bit * HEADS + t] for t in range(HEADS)], axis=1)

    def joined(e):
        wait_near(e)
        wait_far(e)
        quarter = [arrived[e, 4 * q : 4 * q + 4].astype(F32) for q in range(4)]
        total = jnp.concatenate([quarter[0] + quarter[1], quarter[2] + quarter[3]], axis=0)
        return total.reshape(D, TOK).astype(BF16)

    def span(index, size):
        return pl.ds(pl.multiple_of(index * size, size), size)

    def quarters(by_i, one):
        bit = bit_i if by_i else bit_j
        for dx, dy in ((1, 1), (0, 1), (1, 0), (0, 0)):
            quarter = (y + dy - 2 * y * dy) * 2 + (bit + dx - 2 * bit * dx)
            one(quarter, dx, dy)

    lane = lax.broadcasted_iota(jnp.int32, (1, 128), 1)

    def sum_start(n, values):
        tile = jnp.zeros((1, 128), F32)
        for r, value in enumerate(values):
            tile = jnp.where(lane == r, value, tile)
        sum_stage[n, 0] = tile
        sum_lat[n, lat] = tile
        for k in range(1, N_LAT):
            push(
                sum_stage.at[n, 0],
                sum_lat.at[n, lat],
                SUMS + 3 * n,
                {"lat": lax.rem(lat + k, N_LAT)},
            )

    def sum_middle(n):
        drain(sum_lat.at[n, pl.ds(0, N_LAT - 1)], other_recv.at[SUMS + 3 * n])
        tile = jnp.sum(sum_lat[n], axis=0)
        sum_stage[n, 1] = tile
        sum_group[n, slot_i] = tile
        for offset in GROUP_OFFSETS:
            push(
                sum_stage.at[n, 1],
                sum_group.at[n, slot_i],
                SUMS + 3 * n + 1,
                {"lon": member(True, offset)[1]},
            )

    def sum_last(n):
        drain(sum_group.at[n, pl.ds(0, GROUP - 1)], other_recv.at[SUMS + 3 * n + 1])
        sum_stage[n, 2] = jnp.sum(sum_group[n], axis=0)
        push(
            sum_stage.at[n, 2],
            sum_pair.at[n],
            SUMS + 3 * n + 2,
            {"lon": mate_j * 8 + row},
        )

    def sum_end(n, count):
        drain(sum_pair.at[n], other_recv.at[SUMS + 3 * n + 2])
        tile = sum_stage[n, 2] + sum_pair[n]
        return [
            jnp.sum(jnp.where(lane == r, tile, 0.0), axis=1, keepdims=True) for r in range(count)
        ]

    barrier = pltpu.get_barrier_semaphore()

    def greet(target):
        pl.semaphore_signal(barrier, inc=1, device_id=target, device_id_type=MESH)

    for offset in GROUP_OFFSETS:
        greet({"lon": member(True, offset)[1]})
    for offset in GROUP_OFFSETS:
        if offset[0] == 1:
            greet({"lon": member(False, offset)[1]})
    for k in range(1, N_LAT):
        greet({"lat": lax.rem(lat + k, N_LAT)})

    start_loads(
        [
            (prec_hbm, prec_ref),
            (cells_hbm, cells_ref),
            (weights_hbm, weights_ref),
            (innov_hbm, innov_ref),
            (slope_hbm, slope_ref),
            (w_obs_hbm, w_obs_ref),
            (w_down_hbm, w_down_ref),
            (w_out_hbm, w_out_ref),
            (w_up_hbm, w_up_ref),
            (w_value_hbm, w_value_ref),
        ]
    )
    loads[id(key_ref)].wait()
    keys_t = key_ref[...].astype(F32).T.astype(BF16)
    loads[id(query_ref)].wait()
    queries_t = query_ref[...].astype(F32).T.astype(BF16)
    loads[id(prec_ref)].wait()
    prec_t = jnp.broadcast_to(prec_ref[...], (128, CHANNELS)).T
    loads[id(cells_ref)].wait()
    loads[id(weights_ref)].wait()
    loads[id(innov_ref)].wait()
    slot_lane = lax.broadcasted_iota(jnp.int32, (STENCIL, SLOTS), 1)
    for d in range(N_LAT):
        st_stage[d, 0:STENCIL] = cells_ref[0, 0, :, d, :].astype(F32)
        st_stage[d, STENCIL : 2 * STENCIL] = jnp.where(
            slot_lane < count_ref[0, 0, d], weights_ref[0, 0, :, d, :], 0.0
        )
        er_stage[d] = (innov_ref[0, 0, :, d, :] * prec_t).astype(BF16)
    pl.semaphore_wait(barrier, GROUP - 1 + HEADS + N_LAT - 1)
    for k in range(1, N_LAT):
        p = lax.rem(lat + k, N_LAT)
        push(st_stage.at[p], st_arrived.at[lat], STENCILS, {"lat": p})
        push(er_stage.at[p], er_arrived.at[lat], ERRORS, {"lat": p})
    st_arrived[lat] = st_stage[lat]
    er_arrived[lat] = er_stage[lat]
    scatter(KEYS, False, keys_t)
    scatter(QUERIES, True, queries_t)

    loads[id(slope_ref)].wait()
    slope_t[...] = slope_ref[...].astype(F32).T.astype(BF16)
    for ref in (w_obs_ref, w_down_ref, w_out_ref, w_up_ref, w_value_ref):
        loads[id(ref)].wait()

    drain(st_arrived.at[pl.ds(0, N_LAT - 1)], other_recv.at[STENCILS])
    token = lax.broadcasted_iota(jnp.int32, (TOK, SLOTS), 0).astype(F32)
    columns = []
    for a in range(N_LAT):
        rows = st_arrived[a]
        total = jnp.zeros((TOK, SLOTS), F32)
        for k in range(STENCIL):
            total = total + jnp.where(
                token == rows[k : k + 1], rows[STENCIL + k : STENCIL + k + 1], 0.0
            )
        columns.append(total)
    operator = jnp.concatenate(columns, axis=1)
    drain(er_arrived.at[pl.ds(0, N_LAT - 1)], other_recv.at[ERRORS])
    errors = jnp.concatenate([er_arrived[a] for a in range(N_LAT)], axis=1).astype(F32)

    def adjoint_out(grad, e):
        back = (mm(w_do[...], grad) * slope_t[...].astype(F32)).astype(BF16)
        scatter(e, True, (mm(w_ou[...], back) + mm(w_oo[...], grad)).astype(BF16))
        return back

    def adjoint_middle(grad, back):
        middle = mm(w_obs_ref[...], grad) + mm(w_up_ref[...], back)
        return middle, values_of(middle)

    def values_of(middle):
        high = middle.astype(BF16)
        low = (middle - high.astype(F32)).astype(BF16)
        return mm(w_value_t[...], high) + mm(w_value_t[...], low)

    def adjoint_mix(e, back, p):
        wait_near(e)
        upward = (half(e, near).astype(F32) * scale_ref[:, span(near, HALF // 2)]).astype(BF16)
        half_sum[...] = mm(upward, mix[span(near, HALF // 2), :])
        wait_far(e)
        if p == 0:
            set_scale(far, STATS + 1)
        rest = (half(e, far).astype(F32) * scale_ref[:, span(far, HALF // 2)]).astype(BF16)

        def one(quarter, dx, dy):
            cols = span(quarter, HALF // 4)
            half_sum[:, cols] += mm(rest, mix[span(far, HALF // 2), cols])
            for dz in (2, 1, 3, 0):
                piece = half_sum[:, span(quarter * 4 + lax.rem(z + dz, 4), TOK)]
                send_part(back, p, False, (dx, dy, dz), piece.astype(BF16))

        quarters(False, one)

    def tangent_mix(e, back, p):
        wait_near(e)
        half_sum[...] = mm(half(e, near), mix_t[span(near, HALF // 2), :])
        wait_far(e)
        rest = half(e, far)

        def one(quarter, dx, dy):
            cols = span(quarter, HALF // 4)
            out = half_sum[:, cols] + mm(rest, mix_t[span(far, HALF // 2), cols])
            half_sum[:, cols] = out * scale_ref[:, cols]
            for dz in (2, 1, 3, 0):
                piece = half_sum[:, span(quarter * 4 + lax.rem(z + dz, 4), TOK)]
                send_part(back, p, True, (dx, dy, dz), piece.astype(BF16))

        quarters(True, one)

    def tangent_start(v):
        v_in = v.astype(BF16)
        return mm(v_in, w_up_ref[...]), mm(v_in, w_obs_ref[...])

    def tangent_in(started, attended):
        hidden_v, field_v = started
        hidden = hidden_v + mm(attended, w_ou[...])
        hidden = (hidden * slope_ref[...].astype(F32)).astype(BF16)
        field = field_v + mm(attended, w_oo[...]) + mm(hidden, w_do[...])
        grad_t = contract(field, gram, 0, 0, HIGHEST) * prec_t
        return field, grad_t

    grad = contract(errors, operator, 1, 1, HIGHEST).astype(BF16)
    start = mm(w_obs_ref[...], grad)
    back = (mm(w_down_ref[...], start.astype(BF16)) * slope_t[...].astype(F32)).astype(BF16)
    middle = start + mm(w_up_ref[...], back)
    scatter(UP0, True, mm(w_out_ref[...], middle.astype(BF16)).astype(BF16))
    gram = contract(operator, operator, 1, 1, HIGHEST)

    wait_near(KEYS)
    wait_far(KEYS)
    stat_lane = lax.broadcasted_iota(jnp.int32, (TOK, 128), 1)
    keys = jnp.concatenate([arrived[KEYS, t] for t in range(GROUP)], axis=1)
    keys = jnp.concatenate([keys, keys], axis=0)

    def query_of(slot):
        scaled = arrived[QUERIES, slot].astype(F32) * SCORE_SCALE
        high = scaled.astype(BF16)
        low = (scaled - high.astype(F32)).astype(BF16)
        return jnp.concatenate([high, low], axis=0)

    def keys_of(slot):
        return jnp.concatenate([arrived[KEYS, slot], arrived[KEYS, slot]], axis=0)

    def score_rows(slot):
        scores = contract(query_of(slot), keys, 0, 0)
        top = jnp.max(scores, axis=1, keepdims=True)
        raised = jnp.exp2(scores - top)
        total = jnp.sum(raised, axis=1, keepdims=True)
        mix[span(slot, TOK), :] = raised.astype(BF16)
        stat = jnp.where(stat_lane == 0, top, total).T
        stat_mine[:, span(slot, TOK)] = stat[0:8]

    pair = {"lon": mate_i * 8 + row}

    def score_half(bit, sem):
        for t in range(HEADS):
            score_rows(bit * HEADS + t)
        place = span(bit, HALF // 2)
        push(stat_mine.at[:, place], stat_other.at[:, place], sem, pair)

    def set_scale(bit, sem):
        place = span(bit, HALF // 2)
        drain(stat_other.at[:, pl.ds(0, HALF // 2)], other_recv.at[sem])
        top_mine, top_other = stat_mine[0:1, place], stat_other[0:1, place]
        top = jnp.maximum(top_mine, top_other)
        mine = jnp.exp2(top_mine - top)
        scale_ref[:, place] = mine / (
            stat_mine[1:2, place] * mine + stat_other[1:2, place] * jnp.exp2(top_other - top)
        )

    wait_near(QUERIES)
    score_half(near, STATS)
    wait_far(QUERIES)
    score_half(far, STATS + 1)
    set_scale(near, STATS)

    adjoint_mix(UP0, BACK0, 0)

    w_value_t[...] = w_value_ref[...].astype(F32).T.astype(BF16)
    w_vv[...] = mm(w_value_t[...], w_value_ref[...]).astype(BF16)
    middle_values = values_of(middle)
    w_do[...] = mm(w_down_ref[...], w_obs_ref[...]).astype(BF16)
    w_oo[...] = mm(w_out_ref[...], w_obs_ref[...]).astype(BF16)
    w_ou[...] = mm(w_out_ref[...], w_up_ref[...]).astype(BF16)
    spread = joined(BACK0)

    values1 = middle_values + mm(w_vv[...], spread)
    scatter(VAL1, False, values1.astype(BF16))
    queries = jnp.concatenate([query_of(t) for t in range(GROUP)], axis=1)
    for t in range(GROUP):
        mix_t[t * TOK : (t + 1) * TOK, :] = jnp.exp2(
            contract(keys_of(t), queries, 0, 0) - stat_mine[0:1, :]
        ).astype(BF16)
    tangent_mix(VAL1, ATT1, 1)
    r1 = (middle + mm(w_value_ref[...], spread)).T
    rr1 = total_of(r1 * r1)
    started = tangent_start(r1)
    attended = joined(ATT1).astype(F32).T.astype(BF16)
    field, grad_t = tangent_in(started, attended)
    grad = grad_t.astype(BF16)
    grad_1 = grad_t.T
    sum_start(0, [rr1, total_of(field * grad_1)])
    back = adjoint_out(grad, UP1)
    sum_middle(0)
    middle, middle_values = adjoint_middle(grad, back)
    adjoint_mix(UP1, BACK1, 2)
    sum_last(0)
    norm1, seen1 = sum_end(0, 2)
    step1 = norm1 / (norm1 + seen1)
    values2 = values1 - step1 * (values1 + middle_values)
    spread = joined(BACK1)

    values2 = values2 - step1 * mm(w_vv[...], spread)
    scatter(VAL2, False, values2.astype(BF16))
    tangent_mix(VAL2, ATT2, 3)
    applied = r1 + (middle + mm(w_value_ref[...], spread)).T
    r2 = r1 - step1 * applied
    started = tangent_start(r2)
    norms = [total_of(r2 * r2), total_of(r2 * r1)]
    attended = joined(ATT2).astype(F32).T.astype(BF16)
    field, grad_t = tangent_in(started, attended)
    grad = grad_t.astype(BF16)
    sum_start(1, norms + [total_of(field * grad_t.T), total_of(field * grad_1)])
    back = adjoint_out(grad, UP2)
    sum_middle(1)
    partial = r2 + (mm(w_obs_ref[...], grad) + mm(w_up_ref[...], back)).T
    adjoint_mix(UP2, BACK2, 4)
    sum_last(1)
    norm2, cross2, seen2, cross_seen2 = sum_end(1, 4)
    beta = norm2 / norm1
    step2 = norm2 / (
        norm2 + seen2 + 2.0 * beta * (cross2 + cross_seen2) + beta * beta * (norm1 + seen1)
    )
    sol_ref[...] = step1 * r1 + step2 * (r2 + beta * r1)
    partial = r2 - step2 * (partial + beta * applied)
    spread = joined(BACK2)
    res_ref[...] = partial - step2 * mm(w_value_ref[...], spread).T

    for e in range(N_EXCHANGES):
        drain(arrived.at[e, pl.ds(0, GROUP - 1)], send.at[e])
    drain(st_stage.at[pl.ds(0, N_LAT - 1)], other_send.at[STENCILS])
    drain(er_stage.at[pl.ds(0, N_LAT - 1)], other_send.at[ERRORS])
    for k in range(2):
        drain(stat_mine.at[:, pl.ds(0, HALF // 2)], other_send.at[STATS + k])
    for n in range(N_SUMS):
        drain(sum_lat.at[n, pl.ds(0, N_LAT - 1)], other_send.at[SUMS + 3 * n])
        drain(sum_group.at[n, pl.ds(0, GROUP - 1)], other_send.at[SUMS + 3 * n + 1])
        drain(sum_pair.at[n], other_send.at[SUMS + 3 * n + 2])


def per_device(*args):
    args = list(args)
    args[12] = args[12].reshape(1, CHANNELS)
    hbm = pl.BlockSpec(memory_space=pl.ANY)
    vmem = pl.BlockSpec(memory_space=pltpu.VMEM)
    in_specs = [hbm] * 13
    in_specs[10] = pl.BlockSpec(memory_space=pltpu.SMEM)
    return pl.pallas_call(
        kernel,
        out_shape=(pltpu.VMEM((TOK, D), F32),) * 2,
        in_specs=in_specs,
        out_specs=(vmem, vmem),
        scratch_shapes=[
            *[pltpu.VMEM(a.shape, a.dtype) for n, a in enumerate(args) if n != 10],
            pltpu.VMEM((N_EXCHANGES, GROUP, HEAD_DIM, TOK), BF16),
            pltpu.VMEM((N_EXCHANGES, HEADS, HEAD_DIM, TOK), BF16),
            pltpu.VMEM((5, GROUP, HEAD_DIM, TOK), BF16),
            pltpu.VMEM((HEAD_DIM, HALF), F32),
            pltpu.VMEM((HALF, HALF), BF16),
            pltpu.VMEM((HALF, HALF), BF16),
            pltpu.VMEM((8, HALF), F32),
            pltpu.VMEM((8, HALF), F32),
            pltpu.VMEM((1, HALF), F32),
            pltpu.VMEM((FF, TOK), BF16),
            pltpu.VMEM((FF, CHANNELS), BF16),
            pltpu.VMEM((D, CHANNELS), BF16),
            pltpu.VMEM((D, FF), BF16),
            pltpu.VMEM((D, D), BF16),
            pltpu.VMEM((D, D), BF16),
            pltpu.VMEM((N_LAT, 2 * STENCIL, SLOTS), F32),
            pltpu.VMEM((N_LAT, 2 * STENCIL, SLOTS), F32),
            pltpu.VMEM((N_LAT, CHANNELS, SLOTS), BF16),
            pltpu.VMEM((N_LAT, CHANNELS, SLOTS), BF16),
            pltpu.VMEM((N_SUMS, 3, 1, 128), F32),
            pltpu.VMEM((N_SUMS, N_LAT, 1, 128), F32),
            pltpu.VMEM((N_SUMS, GROUP, 1, 128), F32),
            pltpu.VMEM((N_SUMS, 1, 128), F32),
            pltpu.SemaphoreType.DMA((12,)),
            pltpu.SemaphoreType.DMA((N_EXCHANGES,)),
            pltpu.SemaphoreType.DMA((N_EXCHANGES, 2)),
            pltpu.SemaphoreType.DMA((N_OTHER,)),
            pltpu.SemaphoreType.DMA((N_OTHER,)),
        ],
        compiler_params=pltpu.CompilerParams(
            collective_id=0, has_side_effects=True, vmem_limit_bytes=56 * 1024 * 1024
        ),
    )(*args)


def solution(mesh):
    in_specs = (
        P(("lat", "lon"), None),
        P(("lat", "lon"), None),
        P(("lat", "lon"), None),
        P(),
        P(),
        P(),
        P(),
        P(),
        P("lat", "lon", None, None, None),
        P("lat", "lon", None, None, None),
        P("lat", "lon", None),
        P("lat", "lon", None, None, None),
        P(),
    )
    out_specs = (P(("lat", "lon"), None), P(("lat", "lon"), None))
    return jax.shard_map(
        per_device, mesh=mesh, in_specs=in_specs, out_specs=out_specs, check_vma=False
    )
```
